256 devices in a mesh: sx: 4 (over z_lo), sy: 16 (over z_hi, y, core), wn: 4 (over x).
Axes of the slice: x: 4, y: 4, z: 8 (z_hi: 2, z_lo: 4; z = z_hi * 4 + z_lo), core: 2. Of those that a mesh axis runs over, the one named last changes fastest.
Arguments:
- thermal_guess: float32 [16, 64, 32768], P(None, None, ('sx', 'sy', 'wn')), may hold values from -6 to 6
- forcing_vectors: float32 [16, 64, 32768], P(None, None, ('sx', 'sy', 'wn')), may hold values from -4 to 4
- mesh_stack_coordinate: int32 [32768], P(('sx', 'sy', 'wn')), may hold values from 0 to 127, as said below
- self_matrices: bfloat16 [64, 64, 32768], P(None, None, ('sx', 'sy', 'wn')), may hold values from -0.21 to 4
- interface_matrices: bfloat16 [6, 64, 64, 32768], P(None, None, None, ('sx', 'sy', 'wn')), may hold values from -0.19921875 to 0.19921875
- reciprocal_leading_matrices: bfloat16 [64, 64, 32768], P(None, None, ('sx', 'sy', 'wn')), may hold values from -0.04 to 0.34
- beneath_factor_matrices: bfloat16 [64, 64, 32768], P(None, None, ('sx', 'sy', 'wn')), may hold values from -0.1 to 0.1
- overhead_factor_matrices: bfloat16 [64, 64, 32768], P(None, None, ('sx', 'sy', 'wn')), may hold values from -0.1 to 0.1
Outputs:
- new_temperature: float32 [16, 64, 32768], P(None, None, ('sx', 'sy', 'wn'))
The draws below stay inside these ranges and needn't reach their ends.
Inputs may be any that keep to these rules, and one draw needn't show every extreme that they name: `mesh_stack_coordinate`: each aligned block of 128 entries is a permutation of 0 to 127.
All inputs are finite; a program needn't handle non-finite values.
Results may differ from the reference program's by a relative error of at most 0.0057.
Values may be sent and summed in bfloat16 or wider, within the bound.
No kernel may reach another device: no remote copies, remote signals or barrier semaphores. Data moves between devices by JAX's collectives and lax.ppermute only.
A program may use at most 128 MiB of HBM per device.

```python
import jax
import jax.numpy as jnp
from jax import lax

BASIS_SIZE = 64
LOAD_COUNT = 16
LI = 4
LJ = 8
LK = 4
ITERS = 3
LOCAL = 128
LC = 8
NK = 16
NI = 16
NJ = 128
MESH_COUNT = 32768
N_SY = 16
N_WN = 4


def assemble(key, off_values, center_lo, center_hi):
    identity = jnp.eye(BASIS_SIZE, dtype=jnp.float32)[:, :, None]
    center = jax.random.uniform(key, (1, BASIS_SIZE, MESH_COUNT), jnp.float32, center_lo, center_hi)
    return identity * center + (1.0 - identity) * off_values


def shared_signs(key):
    return (2 * jax.random.randint(key, (BASIS_SIZE,), 0, 2) - 1).astype(jnp.float32)


def coherent_block(key):
    sign_vector = shared_signs(key)
    return 0.5 / BASIS_SIZE * sign_vector[:, None, None] * sign_vector[None, :, None]


def draw_mesh_stack_coordinate(key, part):
    key = jax.random.fold_in(key, 5)
    blocks = MESH_COUNT // LOCAL
    scores = jax.random.randint(key, (blocks, LOCAL), 0, 1 << 20) * LOCAL + jnp.arange(LOCAL, dtype=jnp.int32)[None, :]
    return jnp.argsort(scores, axis=1).astype(jnp.int32).reshape(MESH_COUNT)


def draw_self_matrices(key, part):
    key = jax.random.fold_in(key, 1)
    center_key, spread_key = jax.random.split(key)
    off_values = 0.05 * jax.random.truncated_normal(spread_key, -4.0, 4.0, (BASIS_SIZE, BASIS_SIZE, MESH_COUNT), jnp.float32)
    return assemble(center_key, off_values, 3.0, 4.0).astype(jnp.bfloat16)


def draw_reciprocal_leading_matrices(key, part):
    key = jax.random.fold_in(key, 2)
    center_key, spread_key = jax.random.split(key)
    off_values = 0.008 * jax.random.truncated_normal(spread_key, -4.0, 4.0, (BASIS_SIZE, BASIS_SIZE, MESH_COUNT), jnp.float32)
    return assemble(center_key, off_values, 0.25, 0.3333).astype(jnp.bfloat16)


def draw_beneath_factor_matrices(key, part):
    coherent = coherent_block(key)
    key = jax.random.fold_in(key, 6)
    noise_part = 0.02 * jax.random.truncated_normal(key, -3.0, 3.0, (BASIS_SIZE, BASIS_SIZE, MESH_COUNT), jnp.float32)
    return (noise_part + coherent).astype(jnp.bfloat16)


def draw_overhead_factor_matrices(key, part):
    coherent = coherent_block(key)
    key = jax.random.fold_in(key, 7)
    noise_part = 0.02 * jax.random.truncated_normal(key, -3.0, 3.0, (BASIS_SIZE, BASIS_SIZE, MESH_COUNT), jnp.float32)
    return (noise_part - coherent).astype(jnp.bfloat16)


def draw_forcing_vectors(key, part):
    sign_vector = shared_signs(key)
    key = jax.random.fold_in(key, 3)
    value_key, weight_key = jax.random.split(key)
    weights = jax.random.truncated_normal(weight_key, -1.5, 1.5, (LOAD_COUNT, 1, MESH_COUNT), jnp.float32)
    coherent = 1.2 * sign_vector[None, :, None] * weights
    values = 0.7 * jax.random.truncated_normal(value_key, -2.5, 2.5, (LOAD_COUNT, BASIS_SIZE, MESH_COUNT), jnp.float32)
    return values + coherent


def level_of(stream_key, dims, cuts, least, high):
    def one(position, parts):
        steps = jax.random.uniform(jax.random.fold_in(jax.random.fold_in(stream_key, 6), position), (parts,), jnp.float32, least / len(cuts), high / len(cuts))
        return jnp.repeat(jnp.exp(steps), dims[position] // parts).reshape((-1,) + (1,) * (len(dims) - position - 1))

    level = one(*cuts[0])
    for cut in cuts[1:]:
        level = level * one(*cut)
    return level


def noise(own_key, shape, spread, reach, shards=(), kind=jnp.bfloat16):
    factor_of = level_of(own_key, shape, shards, -0.22, 0.18) if shards else 1.0
    drawn = jax.random.normal(own_key, shape, jnp.float32) * spread * factor_of
    return jnp.minimum(jnp.maximum(drawn, -reach), reach).astype(kind)


def setup_inputs(seed: int = 0) -> dict:
    keys = jax.random.split(jax.random.key(seed), 9)
    return {
        "thermal_guess": noise(keys[0], (LOAD_COUNT, BASIS_SIZE, MESH_COUNT), 1.0, 6.0, ((2, 256),), jnp.float32),
        "forcing_vectors": draw_forcing_vectors(jax.random.fold_in(keys[8], 71), 0),
        "mesh_stack_coordinate": draw_mesh_stack_coordinate(jax.random.fold_in(keys[8], 71), 0),
        "self_matrices": draw_self_matrices(jax.random.fold_in(keys[8], 71), 0),
        "interface_matrices": noise(keys[4], (6, BASIS_SIZE, BASIS_SIZE, MESH_COUNT), 0.04, 0.19921875, ((3, 256),)),
        "reciprocal_leading_matrices": draw_reciprocal_leading_matrices(jax.random.fold_in(keys[8], 71), 0),
        "beneath_factor_matrices": draw_beneath_factor_matrices(jax.random.fold_in(keys[8], 71), 0),
        "overhead_factor_matrices": draw_overhead_factor_matrices(jax.random.fold_in(keys[8], 71), 0),
    }


def block_coords(slot_ids):
    block = slot_ids // LOCAL
    first = block // (N_SY * N_WN)
    second = (block // N_WN) % N_SY
    third = block % N_WN
    return first, second, third


def slot_grid(mesh_stack_coordinate):
    total = mesh_stack_coordinate.shape[0]
    slot_ids = jnp.arange(total, dtype=jnp.int32)
    first, second, third = block_coords(slot_ids)
    placing = mesh_stack_coordinate.astype(jnp.int32)
    layer = third * LK + placing // (LI * LJ)
    row_index = first * LI + (placing // LJ) % LI
    col_index = second * LJ + placing % LJ
    return ((layer * NI + row_index) * NJ + col_index).astype(jnp.int32)


def line_grid(total):
    slot_ids = jnp.arange(total, dtype=jnp.int32)
    first, second, third = block_coords(slot_ids)
    local_slot = slot_ids % LOCAL
    layer = local_slot // LC
    column = third * LC + local_slot % LC
    row_index = first * LI + column // LJ
    col_index = second * LJ + column % LJ
    return ((layer * NI + row_index) * NJ + col_index).astype(jnp.int32)


def rounding(values):
    return lax.optimization_barrier(values.astype(jnp.bfloat16)).astype(jnp.float32)


def reference(thermal_guess, forcing_vectors, mesh_stack_coordinate, self_matrices, interface_matrices, reciprocal_leading_matrices, beneath_factor_matrices, overhead_factor_matrices):
    total = mesh_stack_coordinate.shape[0]
    columns = NI * NJ
    grid_index = slot_grid(mesh_stack_coordinate)
    grid_order = jnp.argsort(grid_index).astype(jnp.int32)
    line_order = jnp.argsort(line_grid(total)).astype(jnp.int32)

    def layer_major(factor):
        gathered = jnp.take(factor, line_order, axis=2).reshape(BASIS_SIZE, BASIS_SIZE, NK, columns)
        return jnp.transpose(gathered, (2, 0, 1, 3)).astype(jnp.float32)

    pivots = layer_major(reciprocal_leading_matrices)
    lowers = layer_major(beneath_factor_matrices)
    uppers = layer_major(overhead_factor_matrices)
    diag_wide = self_matrices.astype(jnp.float32)
    present_guess = thermal_guess
    for iteration in range(ITERS):
        widened = rounding(present_guess)
        structured = jnp.take(widened, grid_order, axis=2).reshape(LOAD_COUNT, BASIS_SIZE, NK, NI, NJ)
        padded = jnp.pad(structured, ((0, 0), (0, 0), (1, 1), (1, 1), (1, 1)))
        beside = [padded[:, :, :-2, 1:-1, 1:-1], padded[:, :, 2:, 1:-1, 1:-1],
                  padded[:, :, 1:-1, :-2, 1:-1], padded[:, :, 1:-1, 2:, 1:-1],
                  padded[:, :, 1:-1, 1:-1, :-2], padded[:, :, 1:-1, 1:-1, 2:]]
        residual = forcing_vectors - jnp.einsum('mne,rne->rme', diag_wide, widened)
        for face_index in range(6):
            neighbour = jnp.take(beside[face_index].reshape(LOAD_COUNT, BASIS_SIZE, total), grid_index, axis=2)
            residual = residual - jnp.einsum('mne,rne->rme', interface_matrices[face_index].astype(jnp.float32), neighbour)
        res_wide = rounding(residual)
        line_values = jnp.transpose(jnp.take(res_wide, grid_order, axis=2).reshape(LOAD_COUNT, BASIS_SIZE, NK, columns), (2, 0, 1, 3))
        empty_trace = jnp.zeros((LOAD_COUNT, BASIS_SIZE, columns), jnp.float32)

        def forward(previous, layer_items):
            pivot_layer, lower_layer, source_layer = layer_items
            forward_value = jnp.einsum('mnc,rnc->rmc', pivot_layer, source_layer) - jnp.einsum('mnc,rnc->rmc', lower_layer, previous)
            return rounding(forward_value), forward_value

        _, sweep_values = lax.scan(forward, empty_trace, (pivots, lowers, line_values))

        def backward(following, layer_items):
            upper_layer, forward_value = layer_items
            result = forward_value - jnp.einsum('mnc,rnc->rmc', upper_layer, following)
            return rounding(result), result

        _, solved = lax.scan(backward, empty_trace, (uppers, sweep_values), reverse=True)
        correction = jnp.transpose(solved, (1, 2, 0, 3)).reshape(LOAD_COUNT, BASIS_SIZE, total)
        present_guess = present_guess + jnp.take(correction, grid_index, axis=2)
    return present_guess
```

```python
import jax
import jax.numpy as jnp
from jax import lax
from jax.experimental import pallas as pl
from jax.experimental.pallas import tpu as pltpu
from jax.sharding import PartitionSpec as P

BF = jnp.bfloat16
F32 = jnp.float32
ANY = pl.BlockSpec(memory_space=pl.ANY)
VM = pl.BlockSpec(memory_space=pltpu.VMEM)
SM = pl.BlockSpec(memory_space=pltpu.SMEM)
NT = (((1,), (1,)), ((), ()))


def dot_nt(a, b):
    return lax.dot_general(a, b, NT, preferred_element_type=F32)


def pair_coord(shape, dim):
    p = lax.broadcasted_iota(jnp.int32, shape, dim)
    half, i, k, jp = p // 64, (p // 16) % 4, (p // 4) % 4, p % 4
    return k * 32 + i * 8 + jp + 4 * half


def parts3(x):
    hi = x.astype(BF)
    rest = x - hi.astype(F32)
    mid = rest.astype(BF)
    return hi, mid, (rest - mid.astype(F32)).astype(BF)


PITCH = 132


def t_kernel(msc, selfm, ifc, pm, gm, um, w_out, bp_out, bg_out, bu_out,
             buf, s_ref, stage, in_sem, out_sem):
    sources = [ifc.at[f] for f in range(6)] + [pm, gm, um, selfm]
    copies = []
    for n, source in enumerate(sources):
        copies.append(pltpu.make_async_copy(source, buf.at[n], in_sem.at[n]))
        copies[n].start()
    lo = lax.broadcasted_iota(jnp.int32, (64, 128), 1) < 64
    zero = jnp.zeros((64, 128), BF)

    def turn(a, b):
        @pl.loop(0, 64, unroll=16)
        def _(m):
            rows = jnp.concatenate([buf[a, m], buf[b, m]], axis=0)
            s_ref[pl.ds(m * PITCH, 128), :] = jnp.transpose(rows).astype(F32)

    def picked(s):
        return s_ref[pl.ds(s, 64, stride=PITCH), :].astype(BF)

    def element_rows(s):
        c = msc[s]
        k, i, j = c // 32, (c // 8) % 4, c % 8
        p = ((i * 4 + k) * 4 + j % 4) * 2 + j // 4
        return pl.ds(pl.multiple_of(p * 64, 64), 64)

    def line_rows(s, j):
        p = s - j + (j % 4) * 2 + j // 4
        return pl.ds(pl.multiple_of(p * 64, 64), 64)

    def block(v, rolled, own, half):
        src = v if own == half else rolled
        return jnp.where(lo, src, zero) if half == 0 else jnp.where(lo, zero, src)

    outs = [None] * 7

    def send(n, slot, dst):
        outs[n] = pltpu.make_async_copy(stage.at[slot], dst, out_sem.at[n])
        outs[n].start()

    for t in range(3):
        copies[2 * t].wait()
        copies[2 * t + 1].wait()
        turn(2 * t, 2 * t + 1)

        @pl.loop(0, 128, unroll=16)
        def _(s):
            stage[t, element_rows(s), :] = picked(s)

        send(t, t, w_out.at[t])
    copies[6].wait()
    copies[7].wait()
    turn(6, 7)
    outs[0].wait()

    @pl.loop(0, 16, unroll=2)
    def _(layer):
        for j in range(8):
            v = picked(layer * 8 + j)
            rolled = pltpu.roll(v, 64, 1)
            rows = line_rows(layer * 8 + j, j)
            stage[3, rows, :] = block(v, rolled, 0, j // 4)
            stage[0, rows, :] = block(v, rolled, 1, j // 4)

    send(3, 3, bp_out)
    send(4, 0, bg_out)
    copies[8].wait()
    copies[9].wait()
    turn(8, 9)
    outs[1].wait()
    outs[2].wait()

    @pl.loop(0, 16, unroll=2)
    def _(layer):
        for j in range(8):
            v = picked(layer * 8 + j)
            rolled = pltpu.roll(v, 64, 1) if j // 4 else v
            stage[1, line_rows(layer * 8 + j, j), :] = block(v, rolled, 0, j // 4)
            stage[2, element_rows(layer * 8 + j), :] = jnp.where(lo, zero, v)

    send(5, 1, bu_out)
    send(6, 2, w_out.at[3])
    for n in range(3, 7):
        outs[n].wait()


def transform(msc, selfm, ifc, pm, gm, um):
    blk = jax.ShapeDtypeStruct((8192, 128), BF)
    return pl.pallas_call(
        t_kernel,
        out_shape=(jax.ShapeDtypeStruct((4, 8192, 128), BF), blk, blk, blk),
        in_specs=[SM] + [ANY] * 5,
        out_specs=(ANY,) * 4,
        scratch_shapes=[
            pltpu.VMEM((10, 64, 64, 128), BF),
            pltpu.VMEM((64 * PITCH, 128), F32),
            pltpu.VMEM((4, 8192, 128), BF),
            pltpu.SemaphoreType.DMA((10,)),
            pltpu.SemaphoreType.DMA((7,)),
        ],
        compiler_params=pltpu.CompilerParams(vmem_limit_bytes=48 * 2**20),
        cost_estimate=pl.CostEstimate(flops=0, bytes_accessed=2**25, transcendentals=0),
        name="transform",
    )(msc, selfm, ifc, pm, gm, um)


def s_kernel(r_ref, p_ref, g_ref, u_ref, z_ref, y_ref):
    yb = [None] * 4
    for k in range(16):
        for q in range(4):
            v = dot_nt(r_ref[k, q], p_ref[k * 4 + q])
            if k:
                v = v - dot_nt(yb[q], g_ref[k * 4 + q])
            yb[q] = v.astype(BF)
            y_ref[k, q] = v
    zb = [None] * 4
    for k in reversed(range(16)):
        for q in range(4):
            v = y_ref[k, q]
            if k < 15:
                v = v - dot_nt(zb[q], u_ref[k * 4 + q])
            zb[q] = v.astype(BF)
            for d in range(4):
                w = k - 4 * d + 1
                if 0 <= w < 6:
                    z_ref[d, w, q] = zb[q]
    z_ref[0, 0] = jnp.zeros((4, 16, 128), BF)
    z_ref[3, 5] = jnp.zeros((4, 16, 128), BF)


def solve(r, p, g, u):
    return pl.pallas_call(
        s_kernel,
        out_shape=jax.ShapeDtypeStruct((4, 6, 4, 16, 128), BF),
        in_specs=[VM] * 4,
        out_specs=VM,
        scratch_shapes=[pltpu.VMEM((16, 4, 16, 128), F32)],
        compiler_params=pltpu.CompilerParams(vmem_limit_bytes=48 * 2**20),
        name="solve",
    )(r, p.reshape(64, 128, 128), g.reshape(64, 128, 128), u.reshape(64, 128, 128))


def r_kernel(msk, xb, il, ih, jl, jh, b_ref, w_ref, out_ref, d2):
    g = pl.program_id(0)
    lane = lax.broadcasted_iota(jnp.int32, (16, 128), 1)
    lo = lane < 64

    @pl.when(g == 0)
    def _():
        def keep(n, v):
            return jnp.where(msk[n] > 0, v, jnp.zeros_like(v))

        def put(i, k, j, v, rolled, half):
            d2[i, k, j] = jnp.where(lo, v, rolled) if half == 0 else jnp.where(lo, rolled, v)

        def both(i, k, jp, v):
            r = pltpu.roll(v, 64, 1)
            put(i, k, 1 + jp, v, r, 0)
            put(i, k, 5 + jp, v, r, 1)

        @pl.loop(0, 4)
        def _(i):
            for k in range(6):
                for jp in range(4):
                    both(1 + i, k, jp, xb[i, k, jp])
            for k in range(4):
                v = keep(2, jl[i, k])
                put(1 + i, 1 + k, 0, v, pltpu.roll(v, 64, 1), 1)
                v = keep(3, jh[i, k])
                put(1 + i, 1 + k, 9, v, pltpu.roll(v, 64, 1), 0)

        @pl.loop(0, 4)
        def _(k):
            for jp in range(4):
                both(0, 1 + k, jp, keep(0, il[k, jp]))
                both(5, 1 + k, jp, keep(1, ih[k, jp]))

    i = g // 2
    for kk in range(2):
        k = (g % 2) * 2 + kk
        for jp in range(4):
            rows = []
            for half in range(2):
                j = jp + 4 * half
                ii, k1, jj = i + 1, k + 1, j + 1
                rows.append(jnp.concatenate([
                    jnp.where(lo, d2[ii, k1 - 1, jj], d2[ii, k1 + 1, jj]),
                    jnp.where(lo, d2[ii - 1, k1, jj], d2[ii + 1, k1, jj]),
                    jnp.where(lo, d2[ii, k1, jj - 1], d2[ii, k1, jj + 1]),
                    d2[ii, k1, jj]], axis=1))
            x = jnp.concatenate(rows, axis=0)
            e = (kk * 4 + jp) * 2
            w = jnp.concatenate([w_ref[f, pl.ds(e * 64, 128), :] for f in range(4)], axis=1)
            o = dot_nt(x, w)
            o = jnp.where(lo, o[:16], o[16:])
            out_ref[0, kk, jp] = (b_ref[0, kk, jp] - o).astype(BF)


def residual(msk, xb, il, ih, jl, jh, b, w):
    return pl.pallas_call(
        r_kernel,
        out_shape=jax.ShapeDtypeStruct((4, 4, 4, 16, 128), BF),
        grid=(8,),
        in_specs=[SM, VM, VM, VM, VM, VM,
                  pl.BlockSpec((1, 2, 4, 16, 128), lambda g: (g // 2, g % 2, 0, 0, 0)),
                  pl.BlockSpec((4, 1024, 128), lambda g: (0, g, 0))],
        out_specs=pl.BlockSpec((1, 2, 4, 16, 128), lambda g: (g // 2, g % 2, 0, 0, 0)),
        scratch_shapes=[pltpu.VMEM((6, 6, 10, 16, 128), BF)],
        compiler_params=pltpu.CompilerParams(vmem_limit_bytes=48 * 2**20),
        name="residual",
    )(msk, xb, il, ih, jl, jh, b, w)


def order_kernel(msc, x_ref, *refs):
    outs, s_ref = refs[:-1], refs[-1]
    perm = jnp.where(msc[...] == pair_coord((128, 128), 0), 1.0, 0.0).astype(BF)
    lo = lax.broadcasted_iota(jnp.int32, (64, 128), 1) < 64
    for r in range(16):
        o = None
        for part in parts3(x_ref[r]):
            d = dot_nt(perm, jnp.concatenate([part, part], axis=0))
            o = d if o is None else o + d
        s_ref[pl.ds(r * 68, 64), :] = jnp.where(lo, o[:64], o[64:])
    for i in range(4):
        for k in range(4):
            for jp in range(4):
                v = s_ref[pl.ds((i * 4 + k) * 4 + jp, 16, stride=68), :]
                outs[0][i, k, jp] = v
                if len(outs) > 1:
                    h = v.astype(BF)
                    if k == 0:
                        outs[1][i, jp] = v
                    if k == 3:
                        outs[2][i, jp] = v
                    if i == 0:
                        outs[3][k, jp] = h
                    if i == 3:
                        outs[4][k, jp] = h
                    if jp == 0:
                        outs[5][i, k] = h
                    if jp == 3:
                        outs[6][i, k] = h


def order(msc, x, with_sides):
    own = jax.ShapeDtypeStruct((4, 4, 4, 16, 128), F32)
    wide = jax.ShapeDtypeStruct((4, 4, 16, 128), F32)
    side = jax.ShapeDtypeStruct((4, 4, 16, 128), BF)
    shapes = (own, wide, wide) + (side,) * 4 if with_sides else (own,)
    return pl.pallas_call(
        order_kernel,
        out_shape=shapes,
        in_specs=[VM] * 2,
        out_specs=(VM,) * len(shapes),
        scratch_shapes=[pltpu.VMEM((16 * 68, 128), F32)],
        name="order",
    )(msc, x)


def first_kernel(msk, own, kl, kh, xg_ref, xb_ref):
    for i in range(4):
        for k in range(6):
            if k == 0:
                v = jnp.where(msk[4] > 0, kl[i], jnp.zeros_like(kl[i]))
            elif k == 5:
                v = jnp.where(msk[5] > 0, kh[i], jnp.zeros_like(kh[i]))
            else:
                v = own[i, k - 1]
            xg_ref[i, k] = v
            xb_ref[i, k] = v.astype(BF)


def first(msk, own, kl, kh):
    return pl.pallas_call(
        first_kernel,
        out_shape=(jax.ShapeDtypeStruct((4, 6, 4, 16, 128), F32),
                   jax.ShapeDtypeStruct((4, 6, 4, 16, 128), BF)),
        in_specs=[SM, VM, VM, VM],
        out_specs=(VM, VM),
        name="first",
    )(msk, own, kl, kh)


def update_kernel(z, xg, xo, xb, il, ih, jl, jh):
    for i in range(4):
        for k in range(6):
            v = xg[i, k] + z[i, k].astype(F32)
            h = v.astype(BF)
            xo[i, k] = v
            xb[i, k] = h
            if 0 < k < 5:
                if i == 0:
                    il[k - 1] = h
                if i == 3:
                    ih[k - 1] = h
                jl[i, k - 1] = h[0]
                jh[i, k - 1] = h[3]


def update(z, xg):
    side = jax.ShapeDtypeStruct((4, 4, 16, 128), BF)
    return pl.pallas_call(
        update_kernel,
        out_shape=(jax.ShapeDtypeStruct((4, 6, 4, 16, 128), F32),
                   jax.ShapeDtypeStruct((4, 6, 4, 16, 128), BF)) + (side,) * 4,
        in_specs=[VM] * 2,
        out_specs=(VM,) * 6,
        name="update",
    )(z, xg)


def last_kernel(msc, z, xg, out, s_ref):
    for i in range(4):
        for k in range(4):
            for jp in range(4):
                v = xg[i, k + 1, jp] + z[i, k + 1, jp].astype(F32)
                s_ref[pl.ds(((i * 4 + k) * 4 + jp) * 20, 16), :] = v
    perm = jnp.where(msc[...] == pair_coord((128, 128), 0), 1.0, 0.0).astype(BF)
    for r in range(16):
        v = s_ref[pl.ds(r, 64, stride=20), :]
        t = jnp.transpose(v)
        t = jnp.concatenate([t[:64], t[64:]], axis=1)
        o = None
        for part in parts3(t):
            d = jnp.dot(part, perm, preferred_element_type=F32)
            o = d if o is None else o + d
        out[r] = o


def last(msc, z, xg):
    return pl.pallas_call(
        last_kernel,
        out_shape=jax.ShapeDtypeStruct((16, 64, 128), F32),
        in_specs=[VM] * 3,
        out_specs=VM,
        scratch_shapes=[pltpu.VMEM((64 * 20, 128), F32)],
        name="last",
    )(msc, z, xg)


def shift(x, axis, d):
    n = lax.axis_size(axis)
    return lax.ppermute(x, axis, [(s, (s + d) % n) for s in range(n)])


def body(guess, forcing, msc, selfm, ifc, pm, gm, um):
    edges = []
    for axis in ("sx", "sy", "wn"):
        me = lax.axis_index(axis)
        edges += [me > 0, me < lax.axis_size(axis) - 1]
    msk = jnp.stack(edges).astype(jnp.int32)
    row = msc.reshape(1, 128)
    own, ka, kb, ia, ib, ja, jb = order(row, guess, True)
    kl, kh = shift(kb, "wn", 1), shift(ka, "wn", -1)
    il, ih = shift(ib, "sx", 1), shift(ia, "sx", -1)
    jl, jh = shift(jb, "sy", 1), shift(ja, "sy", -1)
    w, bp, bg, bu = transform(msc, selfm, ifc, pm, gm, um)
    (b,) = order(row, forcing, False)
    xg, xb = first(msk, own, kl, kh)
    for it in range(3):
        res = residual(msk, xb, il, ih, jl, jh, b, w)
        lines = lax.all_to_all(res, "wn", 0, 0, tiled=True)
        z = solve(lines.reshape(16, 4, 16, 128), bp, bg, bu)
        z = lax.all_to_all(z, "wn", 0, 0, tiled=True)
        if it < 2:
            xg, xb, ia, ib, ja, jb = update(z, xg)
            il, ih = shift(ib, "sx", 1), shift(ia, "sx", -1)
            jl, jh = shift(jb, "sy", 1), shift(ja, "sy", -1)
    return last(row, z, xg)


def solution(mesh):
    lastdim = P(None, None, ("sx", "sy", "wn"))
    return jax.shard_map(
        body,
        mesh=mesh,
        in_specs=(lastdim, lastdim, P(("sx", "sy", "wn")), lastdim,
                  P(None, None, None, ("sx", "sy", "wn")), lastdim, lastdim, lastdim),
        out_specs=lastdim,
        check_vma=False,
    )
```

```python
import functools

import jax
import jax.numpy as jnp
from jax import lax
from jax.experimental import pallas as pl
from jax.experimental.pallas import tpu as pltpu
from jax.sharding import PartitionSpec as P

BF = jnp.bfloat16
F32 = jnp.float32
ANY = pl.BlockSpec(memory_space=pl.ANY)
VM = pl.BlockSpec(memory_space=pltpu.VMEM)
SM = pl.BlockSpec(memory_space=pltpu.SMEM)
NT = (((1,), (1,)), ((), ()))


def dot_nt(a, b):
    return lax.dot_general(a, b, NT, preferred_element_type=F32)


def pair_coord(shape, dim):
    p = lax.broadcasted_iota(jnp.int32, shape, dim)
    half, i, k, jp = p // 64, (p // 16) % 4, (p // 4) % 4, p % 4
    return k * 32 + i * 8 + jp + 4 * half


def parts3(x):
    hi = x.astype(BF)
    rest = x - hi.astype(F32)
    mid = rest.astype(BF)
    return hi, mid, (rest - mid.astype(F32)).astype(BF)


PITCH = 132


def t_kernel(msc, selfm, ifc, pm, gm, um, w_out, bp_out, bg_out, bu_out,
             buf, s_ref, stage, lines, in_sem, out_sem):
    sources = [ifc.at[f] for f in range(6)] + [pm, gm, um, selfm]
    copies = []
    for n, source in enumerate(sources):
        copies.append(pltpu.make_async_copy(source, buf.at[n], in_sem.at[n]))
        copies[n].start()
    lo = lax.broadcasted_iota(jnp.int32, (64, 128), 1) < 64
    zero = jnp.zeros((64, 128), BF)

    def turn(a, b):
        @pl.loop(0, 64, unroll=16)
        def _(m):
            rows = jnp.concatenate([buf[a, m], buf[b, m]], axis=0)
            s_ref[pl.ds(m * PITCH, 128), :] = jnp.transpose(rows).astype(F32)

    def picked(s):
        return s_ref[pl.ds(s, 64, stride=PITCH), :].astype(BF)

    def put_element(slot, s, v):
        c = msc[s]
        ik = (((c >> 3) & 3) << 2) | (c >> 5)
        half = pl.multiple_of(((c >> 2) & 1) << 6, 64)
        stage[slot, ik, c & 3, pl.ds(half, 64), :] = v

    outs = [None] * 7

    def send(n, src, dst):
        outs[n] = pltpu.make_async_copy(src, dst, out_sem.at[n])
        outs[n].start()

    for t in range(3):
        copies[2 * t].wait()
        copies[2 * t + 1].wait()
        turn(2 * t, 2 * t + 1)

        @pl.loop(0, 128, unroll=16)
        def _(s):
            put_element(t, s, picked(s))

        send(t, stage.at[t], w_out.at[t])
    copies[6].wait()
    copies[7].wait()
    turn(6, 7)

    @pl.loop(0, 16, unroll=2)
    def _(layer):
        for jp in range(4):
            v0 = picked(layer * 8 + jp)
            v1 = picked(layer * 8 + jp + 4)
            lines[0, layer, jp] = jnp.where(lo, v0, pltpu.roll(v1, 64, 1))
            lines[1, layer, jp] = jnp.where(lo, pltpu.roll(v0, 64, 1), v1)

    send(3, lines.at[0], bp_out)
    send(4, lines.at[1], bg_out)
    copies[8].wait()
    copies[9].wait()
    turn(8, 9)

    @pl.loop(0, 16, unroll=2)
    def _(layer):
        for jp in range(4):
            v0 = picked(layer * 8 + jp)
            v1 = picked(layer * 8 + jp + 4)
            lines[2, layer, jp] = jnp.where(lo, v0, pltpu.roll(v1, 64, 1))
            put_element(3, layer * 8 + jp, jnp.where(lo, zero, v0))
            put_element(3, layer * 8 + jp + 4, jnp.where(lo, zero, v1))

    send(5, lines.at[2], bu_out)
    send(6, stage.at[3], w_out.at[3])
    for n in range(7):
        outs[n].wait()


def transform(msc, selfm, ifc, pm, gm, um):
    blk = jax.ShapeDtypeStruct((16, 4, 64, 128), BF)
    return pl.pallas_call(
        t_kernel,
        out_shape=(jax.ShapeDtypeStruct((4, 16, 4, 128, 128), BF), blk, blk, blk),
        in_specs=[SM] + [ANY] * 5,
        out_specs=(ANY,) * 4,
        scratch_shapes=[
            pltpu.VMEM((10, 64, 64, 128), BF),
            pltpu.VMEM((64 * PITCH, 128), F32),
            pltpu.VMEM((4, 16, 4, 128, 128), BF),
            pltpu.VMEM((3, 16, 4, 64, 128), BF),
            pltpu.SemaphoreType.DMA((10,)),
            pltpu.SemaphoreType.DMA((7,)),
        ],
        compiler_params=pltpu.CompilerParams(vmem_limit_bytes=60 * 2**20),
        cost_estimate=pl.CostEstimate(flops=0, bytes_accessed=2**25, transcendentals=0),
        name="transform",
    )(msc, selfm, ifc, pm, gm, um)


def s_kernel(r_ref, p_ref, g_ref, u_ref, z_ref, y_ref):
    lo = lax.broadcasted_iota(jnp.int32, (64, 128), 1) < 64
    zero = jnp.zeros((64, 128), BF)

    def diag(ref, k, q):
        v = ref[k, q]
        return jnp.concatenate([jnp.where(lo, v, zero), jnp.where(lo, zero, v)], axis=0)

    yb = [None] * 4
    for k in range(16):
        for q in range(4):
            v = dot_nt(r_ref[k, q], diag(p_ref, k, q))
            if k:
                v = v - dot_nt(yb[q], diag(g_ref, k, q))
            yb[q] = v.astype(BF)
            y_ref[k, q] = v
    zb = [None] * 4
    for k in reversed(range(16)):
        for q in range(4):
            v = y_ref[k, q]
            if k < 15:
                v = v - dot_nt(zb[q], diag(u_ref, k, q))
            zb[q] = v.astype(BF)
            for d in range(4):
                w = k - 4 * d + 1
                if 0 <= w < 6:
                    z_ref[d, w, q] = zb[q]
    z_ref[0, 0] = jnp.zeros((4, 16, 128), BF)
    z_ref[3, 5] = jnp.zeros((4, 16, 128), BF)


def solve(r, p, g, u):
    return pl.pallas_call(
        s_kernel,
        out_shape=jax.ShapeDtypeStruct((4, 6, 4, 16, 128), BF),
        in_specs=[VM] * 4,
        out_specs=VM,
        scratch_shapes=[pltpu.VMEM((16, 4, 16, 128), F32)],
        compiler_params=pltpu.CompilerParams(vmem_limit_bytes=24 * 2**20),
        name="solve",
    )(r, p, g, u)


def inner_kernel(msk, *refs, first):
    if first:
        own, kl, kh, b_ref, w_hbm, xo, part, d2, wbuf, sem = refs
    else:
        z, xg, b_ref, w_hbm, xo, part, d2, wbuf, sem = refs
    copies = []
    for i in range(4):
        rows = pl.ds(4 * i, 4)
        copies.append(pltpu.make_async_copy(w_hbm.at[:, rows], wbuf.at[:, rows], sem.at[i]))
        copies[i].start()
    lo = lax.broadcasted_iota(jnp.int32, (16, 128), 1) < 64
    none = jnp.zeros((16, 128), BF)

    @pl.loop(0, 4)
    def _(i):
        for k in range(6):
            for jp in range(4):
                if not first:
                    v = xg[i, k, jp] + z[i, k, jp].astype(F32)
                elif k == 0:
                    v = jnp.where(msk[4] > 0, kl[i, jp], jnp.zeros((16, 128), F32))
                elif k == 5:
                    v = jnp.where(msk[5] > 0, kh[i, jp], jnp.zeros((16, 128), F32))
                else:
                    v = own[i, k - 1, jp]
                xo[i, k, jp] = v
                h = v.astype(BF)
                r = pltpu.roll(h, 64, 1)
                d2[1 + i, k, 1 + jp] = jnp.where(lo, h, r)
                d2[1 + i, k, 5 + jp] = jnp.where(lo, r, h)
            d2[1 + i, k, 0] = none
            d2[1 + i, k, 9] = none
        for k in range(1, 5):
            d2[0, k, 2 * i + 1] = none
            d2[0, k, 2 * i + 2] = none
            d2[5, k, 2 * i + 1] = none
            d2[5, k, 2 * i + 2] = none

    def gathered(i, k, j):
        return jnp.concatenate([
            jnp.where(lo, d2[i, k - 1, j], d2[i, k + 1, j]),
            jnp.where(lo, d2[i - 1, k, j], d2[i + 1, k, j]),
            jnp.where(lo, d2[i, k, j - 1], d2[i, k, j + 1]),
            d2[i, k, j]], axis=1)

    for i in range(4):
        copies[i].wait()
        for k in range(4):
            for jq in range(2):
                x = jnp.concatenate([gathered(i + 1, k + 1, 2 * jq + n + 4 * h + 1)
                                     for n in range(2) for h in range(2)], axis=0)
                w = jnp.concatenate([wbuf[f, 4 * i + k, 2 * jq:2 * jq + 2].reshape(256, 128)
                                     for f in range(4)], axis=1)
                o = dot_nt(x, w)
                for n in range(2):
                    jp = 2 * jq + n
                    cols = slice(128 * n, 128 * n + 128)
                    d = jnp.where(lo, o[32 * n:32 * n + 16, cols], o[32 * n + 16:32 * n + 32, cols])
                    part[i, k, jp] = b_ref[i, k, jp] - d


def inner(msk, state, b, w):
    first = len(state) == 3
    wide = jax.ShapeDtypeStruct((4, 6, 4, 16, 128), F32)
    return pl.pallas_call(
        functools.partial(inner_kernel, first=first),
        out_shape=(wide, jax.ShapeDtypeStruct((4, 4, 4, 16, 128), F32)),
        in_specs=[SM] + [VM] * (len(state) + 1) + [ANY],
        out_specs=(VM, VM),
        scratch_shapes=[pltpu.VMEM((6, 6, 10, 16, 128), BF),
                        pltpu.VMEM((4, 16, 4, 128, 128), BF),
                        pltpu.SemaphoreType.DMA((4,))],
        compiler_params=pltpu.CompilerParams(vmem_limit_bytes=40 * 2**20),
        cost_estimate=pl.CostEstimate(flops=2**27, bytes_accessed=2**24, transcendentals=0),
        name="inner",
    )(msk, *state, b, w)


def outer_kernel(msk, il, ih, jl, jh, part, w_hbm, out, wi, wj, sem):
    copies = []
    for n in range(2):
        copies.append(pltpu.make_async_copy(w_hbm.at[1, pl.ds(12 * n, 4)], wi.at[n], sem.at[n]))
        copies.append(pltpu.make_async_copy(w_hbm.at[2, :, 3 * n], wj.at[n], sem.at[2 + n]))
    for c in copies:
        c.start()
    lo = lax.broadcasted_iota(jnp.int32, (16, 128), 1) < 64
    none = jnp.zeros((16, 128), BF)
    for c in copies:
        c.wait()

    def over_i(n, v, w):
        v = jnp.where(msk[n] > 0, v, none)
        r = pltpu.roll(v, 64, 1)
        if n == 0:
            x = jnp.concatenate([jnp.where(lo, v, none), jnp.where(lo, r, none)], axis=0)
        else:
            x = jnp.concatenate([jnp.where(lo, none, r), jnp.where(lo, none, v)], axis=0)
        o = dot_nt(x, w)
        return jnp.where(lo, o[:16], o[16:])

    def over_j(n, v, w):
        v = jnp.where(msk[2 + n] > 0, v, none)
        r = pltpu.roll(v, 64, 1)
        x = jnp.where(lo, r, none) if n == 0 else jnp.where(lo, none, r)
        o = dot_nt(x, w)
        return jnp.where(lo, o, 0.0) if n == 0 else jnp.where(lo, 0.0, o)

    for i in range(4):
        for k in range(4):
            for jp in range(4):
                v = part[i, k, jp]
                if i == 0:
                    v = v - over_i(0, il[k, jp], wi[0, k, jp])
                if i == 3:
                    v = v - over_i(1, ih[k, jp], wi[1, k, jp])
                if jp == 0:
                    v = v - over_j(0, jl[i, k], wj[0, 4 * i + k])
                if jp == 3:
                    v = v - over_j(1, jh[i, k], wj[1, 4 * i + k])
                out[i, k, jp] = v.astype(BF)


def outer(msk, il, ih, jl, jh, part, w):
    return pl.pallas_call(
        outer_kernel,
        out_shape=jax.ShapeDtypeStruct((4, 4, 4, 16, 128), BF),
        in_specs=[SM] + [VM] * 5 + [ANY],
        out_specs=VM,
        scratch_shapes=[pltpu.VMEM((2, 4, 4, 128, 128), BF),
                        pltpu.VMEM((2, 16, 128, 128), BF),
                        pltpu.SemaphoreType.DMA((4,))],
        compiler_params=pltpu.CompilerParams(vmem_limit_bytes=24 * 2**20),
        name="outer",
    )(msk, il, ih, jl, jh, part, w)


def order_kernel(msc, x_ref, *refs):
    outs, s_ref = refs[:-1], refs[-1]
    perm = jnp.where(msc[...] == pair_coord((128, 128), 0), 1.0, 0.0).astype(BF)
    lo = lax.broadcasted_iota(jnp.int32, (64, 128), 1) < 64
    for r in range(16):
        o = None
        for part in parts3(x_ref[r]):
            d = dot_nt(perm, jnp.concatenate([part, part], axis=0))
            o = d if o is None else o + d
        s_ref[pl.ds(r * 68, 64), :] = jnp.where(lo, o[:64], o[64:])
    for i in range(4):
        for k in range(4):
            for jp in range(4):
                v = s_ref[pl.ds((i * 4 + k) * 4 + jp, 16, stride=68), :]
                outs[0][i, k, jp] = v
                if len(outs) > 1:
                    h = v.astype(BF)
                    if k == 0:
                        outs[1][i, jp] = v
                    if k == 3:
                        outs[2][i, jp] = v
                    if i == 0:
                        outs[3][k, jp] = h
                    if i == 3:
                        outs[4][k, jp] = h
                    if jp == 0:
                        outs[5][i, k] = h
                    if jp == 3:
                        outs[6][i, k] = h


def order(msc, x, with_sides):
    own = jax.ShapeDtypeStruct((4, 4, 4, 16, 128), F32)
    wide = jax.ShapeDtypeStruct((4, 4, 16, 128), F32)
    side = jax.ShapeDtypeStruct((4, 4, 16, 128), BF)
    shapes = (own, wide, wide) + (side,) * 4 if with_sides else (own,)
    return pl.pallas_call(
        order_kernel,
        out_shape=shapes,
        in_specs=[VM] * 2,
        out_specs=(VM,) * len(shapes),
        scratch_shapes=[pltpu.VMEM((16 * 68, 128), F32)],
        name="order",
    )(msc, x)


def sides_kernel(z, xg, ia, ib, ja, jb, xi, xj, sem):
    layers = pl.ds(1, 4)
    copies = []
    for n in range(2):
        copies.append(pltpu.make_async_copy(xg.at[3 * n, layers], xi.at[n], sem.at[n]))
        copies.append(pltpu.make_async_copy(xg.at[:, layers, 3 * n], xj.at[n], sem.at[2 + n]))
    for c in copies:
        c.start()
    for c in copies:
        c.wait()
    for n in range(2):
        (ia, ib)[n][...] = (xi[n] + z[3 * n, 1:5].astype(F32)).astype(BF)
        (ja, jb)[n][...] = (xj[n] + z[:, 1:5, 3 * n].astype(F32)).astype(BF)


def sides(z, xg):
    side = jax.ShapeDtypeStruct((4, 4, 16, 128), BF)
    return pl.pallas_call(
        sides_kernel,
        out_shape=(side,) * 4,
        in_specs=[VM, ANY],
        out_specs=(VM,) * 4,
        scratch_shapes=[pltpu.VMEM((2, 4, 4, 16, 128), F32)] * 2 + [pltpu.SemaphoreType.DMA((4,))],
        compiler_params=pltpu.CompilerParams(vmem_limit_bytes=24 * 2**20),
        name="sides",
    )(z, xg)


def last_kernel(msc, z, xg, out, s_ref):
    for i in range(4):
        for k in range(4):
            for jp in range(4):
                v = xg[i, k + 1, jp] + z[i, k + 1, jp].astype(F32)
                s_ref[pl.ds(((i * 4 + k) * 4 + jp) * 20, 16), :] = v
    perm = jnp.where(msc[...] == pair_coord((128, 128), 0), 1.0, 0.0).astype(BF)
    for r in range(16):
        v = s_ref[pl.ds(r, 64, stride=20), :]
        t = jnp.transpose(v)
        t = jnp.concatenate([t[:64], t[64:]], axis=1)
        o = None
        for part in parts3(t):
            d = jnp.dot(part, perm, preferred_element_type=F32)
            o = d if o is None else o + d
        out[r] = o


def last(msc, z, xg):
    return pl.pallas_call(
        last_kernel,
        out_shape=jax.ShapeDtypeStruct((16, 64, 128), F32),
        in_specs=[VM] * 3,
        out_specs=VM,
        scratch_shapes=[pltpu.VMEM((64 * 20, 128), F32)],
        name="last",
    )(msc, z, xg)


def shift(x, axis, d):
    n = lax.axis_size(axis)
    return lax.ppermute(x, axis, [(s, (s + d) % n) for s in range(n)])


def body(guess, forcing, msc, selfm, ifc, pm, gm, um):
    edges = []
    for axis in ("sx", "sy", "wn"):
        me = lax.axis_index(axis)
        edges += [me > 0, me < lax.axis_size(axis) - 1]
    msk = jnp.stack(edges).astype(jnp.int32)
    row = msc.reshape(1, 128)
    own, ka, kb, ia, ib, ja, jb = order(row, guess, True)
    kl, kh = shift(kb, "wn", 1), shift(ka, "wn", -1)
    il, ih = shift(ib, "sx", 1), shift(ia, "sx", -1)
    jl, jh = shift(jb, "sy", 1), shift(ja, "sy", -1)
    w, bp, bg, bu = transform(msc, selfm, ifc, pm, gm, um)
    (b,) = order(row, forcing, False)
    state = (own, kl, kh)
    for it in range(3):
        xg, part = inner(msk, state, b, w)
        res = outer(msk, il, ih, jl, jh, part, w)
        lines = lax.all_to_all(res, "wn", 0, 0, tiled=True)
        z = solve(lines.reshape(16, 4, 16, 128), bp, bg, bu)
        z = lax.all_to_all(z, "wn", 0, 0, tiled=True)
        if it < 2:
            ia, ib, ja, jb = sides(z, xg)
            il, ih = shift(ib, "sx", 1), shift(ia, "sx", -1)
            jl, jh = shift(jb, "sy", 1), shift(ja, "sy", -1)
            state = (z, xg)
    return last(row, z, xg)


def solution(mesh):
    lastdim = P(None, None, ("sx", "sy", "wn"))
    return jax.shard_map(
        body,
        mesh=mesh,
        in_specs=(lastdim, lastdim, P(("sx", "sy", "wn")), lastdim,
                  P(None, None, None, ("sx", "sy", "wn")), lastdim, lastdim, lastdim),
        out_specs=lastdim,
        check_vma=False,
    )
```

```python
import functools

import jax
import jax.numpy as jnp
from jax import lax
from jax.experimental import pallas as pl
from jax.experimental.pallas import tpu as pltpu
from jax.sharding import PartitionSpec as P

BF = jnp.bfloat16
F32 = jnp.float32
ANY = pl.BlockSpec(memory_space=pl.ANY)
VM = pl.BlockSpec(memory_space=pltpu.VMEM)
SM = pl.BlockSpec(memory_space=pltpu.SMEM)
NT = (((1,), (1,)), ((), ()))


def dot_nt(a, b):
    return lax.dot_general(a, b, NT, preferred_element_type=F32)


PITCH = 132


def turn(buf, s_ref, a, b):
    @pl.loop(0, 64, unroll=16)
    def _(m):
        rows = jnp.concatenate([buf[a, m], buf[b, m]], axis=0)
        s_ref[pl.ds(m * PITCH, 128), :] = jnp.transpose(rows).astype(F32)


def picked(s_ref, s):
    return s_ref[pl.ds(s, 64, stride=PITCH), :].astype(BF)


def fetch(sources, buf, sem):
    copies = []
    for n, source in enumerate(sources):
        copies.append(pltpu.make_async_copy(source, buf.at[n], sem.at[n]))
        copies[n].start()
    return copies


def elements_kernel(msc, selfm, ifc, w_out, buf, s_ref, sem):
    copies = fetch([ifc.at[f] for f in range(6)] + [selfm], buf, sem)
    lo = lax.broadcasted_iota(jnp.int32, (64, 128), 1) < 64
    zero = jnp.zeros((64, 128), BF)
    for t in range(4):
        a, b = (2 * t, 2 * t + 1) if t < 3 else (6, 6)
        copies[a].wait()
        if a != b:
            copies[b].wait()
        turn(buf, s_ref, a, b)

        @pl.loop(0, 128, unroll=16)
        def _(s):
            c = msc[s]
            ik = (((c >> 3) & 3) << 2) | (c >> 5)
            half = pl.multiple_of(((c >> 2) & 1) << 6, 64)
            v = picked(s_ref, s)
            w_out[t, ik, c & 3, pl.ds(half, 64), :] = v if t < 3 else jnp.where(lo, zero, v)


def elements(msc, selfm, ifc):
    return pl.pallas_call(
        elements_kernel,
        out_shape=jax.ShapeDtypeStruct((4, 16, 4, 128, 128), BF),
        in_specs=[SM, ANY, ANY],
        out_specs=VM,
        scratch_shapes=[
            pltpu.VMEM((7, 64, 64, 128), BF),
            pltpu.VMEM((64 * PITCH, 128), F32),
            pltpu.SemaphoreType.DMA((7,)),
        ],
        compiler_params=pltpu.CompilerParams(vmem_limit_bytes=24 * 2**20),
        cost_estimate=pl.CostEstimate(flops=0, bytes_accessed=2**25, transcendentals=0),
        name="elements",
    )(msc, selfm, ifc)


def lines_kernel(pm, gm, um, out, buf, s_ref, sem):
    copies = fetch([pm, gm, um], buf, sem)
    lo = lax.broadcasted_iota(jnp.int32, (64, 128), 1) < 64
    copies[0].wait()
    copies[1].wait()
    turn(buf, s_ref, 0, 1)

    @pl.loop(0, 16, unroll=2)
    def _(layer):
        for jp in range(4):
            v0 = picked(s_ref, layer * 8 + jp)
            v1 = picked(s_ref, layer * 8 + jp + 4)
            out[0, layer, jp] = jnp.where(lo, v0, pltpu.roll(v1, 64, 1))
            out[1, layer, jp] = jnp.where(lo, pltpu.roll(v0, 64, 1), v1)

    copies[2].wait()
    turn(buf, s_ref, 2, 2)

    @pl.loop(0, 16, unroll=2)
    def _(layer):
        for jp in range(4):
            out[2, layer, jp] = jnp.where(lo, picked(s_ref, layer * 8 + jp), picked(s_ref, layer * 8 + jp + 4))


def factors(pm, gm, um):
    return pl.pallas_call(
        lines_kernel,
        out_shape=jax.ShapeDtypeStruct((3, 16, 4, 64, 128), BF),
        in_specs=[ANY] * 3,
        out_specs=VM,
        scratch_shapes=[
            pltpu.VMEM((3, 64, 64, 128), BF),
            pltpu.VMEM((64 * PITCH, 128), F32),
            pltpu.SemaphoreType.DMA((3,)),
        ],
        compiler_params=pltpu.CompilerParams(vmem_limit_bytes=16 * 2**20),
        cost_estimate=pl.CostEstimate(flops=0, bytes_accessed=2**24, transcendentals=0),
        name="factors",
    )(pm, gm, um)


def s_kernel(r_ref, f_ref, z_ref, y_ref):
    lo = lax.broadcasted_iota(jnp.int32, (64, 128), 1) < 64
    zero = jnp.zeros((64, 128), BF)

    def diag(n, k, q):
        v = f_ref[n, k, q]
        return jnp.concatenate([jnp.where(lo, v, zero), jnp.where(lo, zero, v)], axis=0)

    yb = [None] * 4
    for k in range(16):
        for q in range(4):
            v = dot_nt(r_ref[k, q], diag(0, k, q))
            if k:
                v = v - dot_nt(yb[q], diag(1, k, q))
            yb[q] = v.astype(BF)
            y_ref[k, q] = v
    zb = [None] * 4
    for k in reversed(range(16)):
        for q in range(4):
            v = y_ref[k, q]
            if k < 15:
                v = v - dot_nt(zb[q], diag(2, k, q))
            zb[q] = v.astype(BF)
            for d in range(4):
                w = k - 4 * d + 1
                if 0 <= w < 6:
                    z_ref[d, w, q] = zb[q]
    z_ref[0, 0] = jnp.zeros((4, 16, 128), BF)
    z_ref[3, 5] = jnp.zeros((4, 16, 128), BF)


def solve(r, f):
    return pl.pallas_call(
        s_kernel,
        out_shape=jax.ShapeDtypeStruct((4, 6, 4, 16, 128), BF),
        in_specs=[VM] * 2,
        out_specs=VM,
        scratch_shapes=[pltpu.VMEM((16, 4, 16, 128), F32)],
        compiler_params=pltpu.CompilerParams(vmem_limit_bytes=16 * 2**20),
        name="solve",
    )(r, f)


def inner_kernel(*refs, first):
    if first:
        own, kl, kh, b_ref, wbuf, xo, d2 = refs
    else:
        z, xg, b_ref, wbuf, xo, d2 = refs
    msk = inside()
    lo = lax.broadcasted_iota(jnp.int32, (16, 128), 1) < 64
    none = jnp.zeros((16, 128), BF)

    @pl.loop(0, 4)
    def _(i):
        for k in range(6):
            for jp in range(4):
                if not first:
                    v = xg[i, k, jp] + z[i, k, jp].astype(F32)
                elif k == 0:
                    v = jnp.where(msk[4], kl[i, jp], jnp.zeros((16, 128), F32))
                elif k == 5:
                    v = jnp.where(msk[5], kh[i, jp], jnp.zeros((16, 128), F32))
                else:
                    v = own[i, k - 1, jp]
                xo[i, k, jp] = v
                h = v.astype(BF)
                r = pltpu.roll(h, 64, 1)
                d2[1 + i, k, 1 + jp] = jnp.where(lo, h, r)
                d2[1 + i, k, 5 + jp] = jnp.where(lo, r, h)
            d2[1 + i, k, 0] = none
            d2[1 + i, k, 9] = none
        for k in range(1, 5):
            d2[0, k, 2 * i + 1] = none
            d2[0, k, 2 * i + 2] = none
            d2[5, k, 2 * i + 1] = none
            d2[5, k, 2 * i + 2] = none

    def gathered(i, k, j):
        return jnp.concatenate([
            jnp.where(lo, d2[i, k - 1, j], d2[i, k + 1, j]),
            jnp.where(lo, d2[i - 1, k, j], d2[i + 1, k, j]),
            jnp.where(lo, d2[i, k, j - 1], d2[i, k, j + 1]),
            d2[i, k, j]], axis=1)

    for i in range(4):
        for k in range(4):
            for jq in range(2):
                x = jnp.concatenate([gathered(i + 1, k + 1, 2 * jq + n + 4 * h + 1)
                                     for n in range(2) for h in range(2)], axis=0)
                w = jnp.concatenate([wbuf[f, 4 * i + k, 2 * jq:2 * jq + 2].reshape(256, 128)
                                     for f in range(4)], axis=1)
                o = dot_nt(x, w)
                for n in range(2):
                    jp = 2 * jq + n
                    cols = slice(128 * n, 128 * n + 128)
                    d = jnp.where(lo, o[32 * n:32 * n + 16, cols], o[32 * n + 16:32 * n + 32, cols])
                    xo[i, 6 + k, jp] = b_ref[i, k, jp] - d


def inner(state, b, w):
    first = len(state) == 3
    return pl.pallas_call(
        functools.partial(inner_kernel, first=first),
        out_shape=jax.ShapeDtypeStruct((4, 10, 4, 16, 128), F32),
        in_specs=[VM] * (len(state) + 2),
        out_specs=VM,
        scratch_shapes=[pltpu.VMEM((6, 6, 10, 16, 128), BF)],
        compiler_params=pltpu.CompilerParams(vmem_limit_bytes=24 * 2**20),
        cost_estimate=pl.CostEstimate(flops=2**27, bytes_accessed=2**24, transcendentals=0),
        name="inner",
    )(*state, b, w)


def outer_kernel(il, ih, jl, jh, part, w, out):
    msk = inside()
    lo = lax.broadcasted_iota(jnp.int32, (16, 128), 1) < 64
    none = jnp.zeros((16, 128), BF)

    def over_i(n, v, w):
        v = jnp.where(msk[n], v, none)
        r = pltpu.roll(v, 64, 1)
        if n == 0:
            x = jnp.concatenate([jnp.where(lo, v, none), jnp.where(lo, r, none)], axis=0)
        else:
            x = jnp.concatenate([jnp.where(lo, none, r), jnp.where(lo, none, v)], axis=0)
        o = dot_nt(x, w)
        return jnp.where(lo, o[:16], o[16:])

    def over_j(n, v, w):
        v = jnp.where(msk[2 + n], v, none)
        r = pltpu.roll(v, 64, 1)
        x = jnp.where(lo, r, none) if n == 0 else jnp.where(lo, none, r)
        o = dot_nt(x, w)
        return jnp.where(lo, o, 0.0) if n == 0 else jnp.where(lo, 0.0, o)

    for i in range(4):
        for k in range(4):
            for jp in range(4):
                v = part[i, 6 + k, jp]
                if i == 0:
                    v = v - over_i(0, il[k, jp], w[1, k, jp])
                if i == 3:
                    v = v - over_i(1, ih[k, jp], w[1, 12 + k, jp])
                if jp == 0:
                    v = v - over_j(0, jl[i, k], w[2, 4 * i + k, 0])
                if jp == 3:
                    v = v - over_j(1, jh[i, k], w[2, 4 * i + k, 3])
                out[i, k, jp] = v.astype(BF)


def outer(il, ih, jl, jh, part, w):
    return pl.pallas_call(
        outer_kernel,
        out_shape=jax.ShapeDtypeStruct((4, 4, 4, 16, 128), BF),
        in_specs=[VM] * 6,
        out_specs=VM,
        compiler_params=pltpu.CompilerParams(vmem_limit_bytes=24 * 2**20),
        name="outer",
    )(il, ih, jl, jh, part, w)


def inside():
    edges = []
    for axis in ("sx", "sy", "wn"):
        me = lax.axis_index(axis)
        edges += [me > 0, me < lax.axis_size(axis) - 1]
    return edges


def places(msc, inv):
    @pl.loop(0, 128, unroll=8)
    def _(s):
        inv[msc[s]] = s

    def slot(i, k, j):
        return inv[k * 32 + i * 8 + j]

    return slot


def order_kernel(msc, x_ref, *refs):
    outs, s_ref, inv = refs[:-2], refs[-2], refs[-1]
    slot = places(msc, inv)
    lo = lax.broadcasted_iota(jnp.int32, (16, 128), 1) < 64
    for r in range(16):
        x = x_ref[r]
        s_ref[pl.ds(r * PITCH, 128), :] = jnp.transpose(jnp.concatenate([x, x], axis=0))
    for i in range(4):
        for k in range(4):
            for jp in range(4):
                v = jnp.where(lo, s_ref[pl.ds(slot(i, k, jp), 16, stride=PITCH), :],
                              s_ref[pl.ds(slot(i, k, jp + 4), 16, stride=PITCH), :])
                outs[0][i, k, jp] = v
                if len(outs) > 1:
                    h = v.astype(BF)
                    if k == 0:
                        outs[1][i, jp] = v
                    if k == 3:
                        outs[2][i, jp] = v
                    if i == 0:
                        outs[3][k, jp] = h
                    if i == 3:
                        outs[4][k, jp] = h
                    if jp == 0:
                        outs[5][i, k] = h
                    if jp == 3:
                        outs[6][i, k] = h


def order(msc, x, with_sides):
    own = jax.ShapeDtypeStruct((4, 4, 4, 16, 128), F32)
    wide = jax.ShapeDtypeStruct((4, 4, 16, 128), F32)
    side = jax.ShapeDtypeStruct((4, 4, 16, 128), BF)
    shapes = (own, wide, wide) + (side,) * 4 if with_sides else (own,)
    return pl.pallas_call(
        order_kernel,
        out_shape=shapes,
        in_specs=[SM, VM],
        out_specs=(VM,) * len(shapes),
        scratch_shapes=[pltpu.VMEM((16 * PITCH, 128), F32), pltpu.SMEM((128,), jnp.int32)],
        compiler_params=pltpu.CompilerParams(vmem_limit_bytes=8 * 2**20),
        name="order",
    )(msc, x)


def sides_kernel(z, xg, ia, ib, ja, jb):
    for n in range(2):
        (ia, ib)[n][...] = (xg[3 * n, 1:5] + z[3 * n, 1:5].astype(F32)).astype(BF)
        (ja, jb)[n][...] = (xg[:, 1:5, 3 * n] + z[:, 1:5, 3 * n].astype(F32)).astype(BF)


def sides(z, xg):
    side = jax.ShapeDtypeStruct((4, 4, 16, 128), BF)
    return pl.pallas_call(
        sides_kernel,
        out_shape=(side,) * 4,
        in_specs=[VM, VM],
        out_specs=(VM,) * 4,
        compiler_params=pltpu.CompilerParams(vmem_limit_bytes=24 * 2**20),
        name="sides",
    )(z, xg)


def last_kernel(msc, row, z, xg, out, s_ref, inv):
    slot = places(msc, inv)
    for i in range(4):
        for k in range(4):
            for jp in range(4):
                v = xg[i, k + 1, jp] + z[i, k + 1, jp].astype(F32)
                s_ref[pl.ds(slot(i, k, jp), 16, stride=PITCH), :] = v
                s_ref[pl.ds(slot(i, k, jp + 4), 16, stride=PITCH), :] = v
    low = jnp.broadcast_to((row[...] & 4) == 0, (64, 128))
    for r in range(16):
        t = jnp.transpose(s_ref[pl.ds(r * PITCH, 128), :])
        out[r] = jnp.where(low, t[:64], t[64:])


def last(msc, row, z, xg):
    return pl.pallas_call(
        last_kernel,
        out_shape=jax.ShapeDtypeStruct((16, 64, 128), F32),
        in_specs=[SM] + [VM] * 3,
        out_specs=VM,
        scratch_shapes=[pltpu.VMEM((16 * PITCH, 128), F32), pltpu.SMEM((128,), jnp.int32)],
        compiler_params=pltpu.CompilerParams(vmem_limit_bytes=8 * 2**20),
        name="last",
    )(msc, row, z, xg)


def shift(x, axis, d):
    n = lax.axis_size(axis)
    return lax.ppermute(x, axis, [(s, (s + d) % n) for s in range(n)])


def body(guess, forcing, msc, selfm, ifc, pm, gm, um):
    row = msc.reshape(1, 128)
    own, ka, kb, ia, ib, ja, jb = order(msc, guess, True)
    kl, kh = shift(kb, "wn", 1), shift(ka, "wn", -1)
    il, ih = shift(ib, "sx", 1), shift(ia, "sx", -1)
    jl, jh = shift(jb, "sy", 1), shift(ja, "sy", -1)
    w = elements(msc, selfm, ifc)
    f = factors(pm, gm, um)
    w, f = lax.optimization_barrier((w, f))
    (b,) = order(msc, forcing, False)
    state = (own, kl, kh)
    for it in range(3):
        xg = inner(state, b, w)
        res = outer(il, ih, jl, jh, xg, w)
        lines = lax.all_to_all(res, "wn", 0, 0, tiled=True)
        z = solve(lines.reshape(16, 4, 16, 128), f)
        z = lax.all_to_all(z, "wn", 0, 0, tiled=True)
        if it < 2:
            ia, ib, ja, jb = sides(z, xg)
            il, ih = shift(ib, "sx", 1), shift(ia, "sx", -1)
            jl, jh = shift(jb, "sy", 1), shift(ja, "sy", -1)
            state = (z, xg)
    return last(msc, row, z, xg)


def solution(mesh):
    lastdim = P(None, None, ("sx", "sy", "wn"))
    return jax.shard_map(
        body,
        mesh=mesh,
        in_specs=(lastdim, lastdim, P(("sx", "sy", "wn")), lastdim,
                  P(None, None, None, ("sx", "sy", "wn")), lastdim, lastdim, lastdim),
        out_specs=lastdim,
        check_vma=False,
    )
```

```python
import functools

import jax
import jax.numpy as jnp
from jax import lax
from jax.experimental import pallas as pl
from jax.experimental.pallas import tpu as pltpu
from jax.sharding import PartitionSpec as P

BF = jnp.bfloat16
F32 = jnp.float32
VM = pl.BlockSpec(memory_space=pltpu.VMEM)
HBM = pl.BlockSpec(memory_space=pltpu.HBM)
NT = (((1,), (1,)), ((), ()))


def in_hbm(*arrays):
    return [pltpu.with_memory_space_constraint(a, pltpu.HBM) for a in arrays]


def dot_nt(a, b):
    return lax.dot_general(a, b, NT, preferred_element_type=F32)


PITCH = 132


def turn(buf, s_ref, a, b):
    @pl.loop(0, 64, unroll=32)
    def _(m):
        rows = jnp.concatenate([buf[a, m], buf[b, m]], axis=0)
        s_ref[pl.ds(m * PITCH, 128), :] = jnp.transpose(rows).astype(F32)


def picked(s_ref, s):
    return s_ref[pl.ds(s, 64, stride=PITCH), :].astype(BF)


def places(msc, inv):
    @pl.loop(0, 128, unroll=8)
    def _(s):
        inv[msc[s]] = s

    def slot(i, k, j):
        return inv[k * 32 + i * 8 + j]

    return slot


def spread(x_ref, s_ref):
    for r in range(16):
        x = x_ref[r]
        s_ref[pl.ds(r * PITCH, 128), :] = jnp.transpose(jnp.concatenate([x, x], axis=0))


def paired(s_ref, slot, i, k, jp, lo):
    return jnp.where(lo, s_ref[pl.ds(slot(i, k, jp), 16, stride=PITCH), :],
                     s_ref[pl.ds(slot(i, k, jp + 4), 16, stride=PITCH), :])


def prepare_kernel(msc_hbm, x_hbm, selfm, ifc, pm, gm, um, b_out, w_out, f_out,
                   msc, inv, x_ref, buf, s_ref, sem):
    sources = [ifc.at[f] for f in range(6)] + [pm, selfm, gm, um]
    copies = [pltpu.make_async_copy(s, buf.at[n], sem.at[n]) for n, s in enumerate(sources)]
    to_msc = pltpu.make_async_copy(msc_hbm, msc, sem.at[10])
    to_x = pltpu.make_async_copy(x_hbm, x_ref, sem.at[11])
    for c in [to_msc, to_x] + copies:
        c.start()
    lo16 = lax.broadcasted_iota(jnp.int32, (16, 128), 1) < 64
    lo = lax.broadcasted_iota(jnp.int32, (64, 128), 1) < 64
    zero = jnp.zeros((64, 128), BF)
    to_msc.wait()
    slot = places(msc, inv)
    to_x.wait()
    spread(x_ref, s_ref)
    for i in range(4):
        for k in range(4):
            for jp in range(4):
                b_out[i, k, jp] = paired(s_ref, slot, i, k, jp, lo16)

    def put_element(t, s, v):
        c = msc[s]
        ik = (((c >> 3) & 3) << 2) | (c >> 5)
        half = pl.multiple_of(((c >> 2) & 1) << 6, 64)
        w_out[t, ik, c & 3, pl.ds(half, 64), :] = v

    for t in range(3):
        copies[2 * t].wait()
        copies[2 * t + 1].wait()
        turn(buf, s_ref, 2 * t, 2 * t + 1)

        @pl.loop(0, 128, unroll=16)
        def _(s):
            put_element(t, s, picked(s_ref, s))

    copies[6].wait()
    copies[7].wait()
    turn(buf, s_ref, 6, 7)

    @pl.loop(0, 16, unroll=2)
    def _(layer):
        for jp in range(4):
            v0 = picked(s_ref, layer * 8 + jp)
            v1 = picked(s_ref, layer * 8 + jp + 4)
            f_out[0, layer, jp] = jnp.where(lo, v0, pltpu.roll(v1, 64, 1))
            put_element(3, layer * 8 + jp, jnp.where(lo, zero, v0))
            put_element(3, layer * 8 + jp + 4, jnp.where(lo, zero, v1))

    copies[8].wait()
    copies[9].wait()
    turn(buf, s_ref, 8, 9)

    @pl.loop(0, 16, unroll=2)
    def _(layer):
        for jp in range(4):
            v0 = picked(s_ref, layer * 8 + jp)
            v1 = picked(s_ref, layer * 8 + jp + 4)
            f_out[1, layer, jp] = jnp.where(lo, v0, pltpu.roll(v1, 64, 1))
            f_out[2, layer, jp] = jnp.where(lo, pltpu.roll(v0, 64, 1), v1)


def prepare(msc, x, selfm, ifc, pm, gm, um):
    return pl.pallas_call(
        prepare_kernel,
        out_shape=(jax.ShapeDtypeStruct((4, 4, 4, 16, 128), F32),
                   jax.ShapeDtypeStruct((4, 16, 4, 128, 128), BF),
                   jax.ShapeDtypeStruct((3, 16, 4, 64, 128), BF)),
        in_specs=[HBM] * 7,
        out_specs=(VM,) * 3,
        scratch_shapes=[
            pltpu.SMEM((128,), jnp.int32),
            pltpu.SMEM((128,), jnp.int32),
            pltpu.VMEM((16, 64, 128), F32),
            pltpu.VMEM((10, 64, 64, 128), BF),
            pltpu.VMEM((64 * PITCH, 128), F32),
            pltpu.SemaphoreType.DMA((12,)),
        ],
        compiler_params=pltpu.CompilerParams(vmem_limit_bytes=20 * 2**20),
        cost_estimate=pl.CostEstimate(flops=0, bytes_accessed=2**25, transcendentals=0),
        name="prepare",
    )(*in_hbm(msc, x, selfm, ifc, pm, gm, um))


def s_kernel(r_ref, f_ref, z_ref, y_ref):
    lo = lax.broadcasted_iota(jnp.int32, (64, 128), 1) < 64
    zero = jnp.zeros((64, 128), BF)

    def diag(n, k, q):
        v = f_ref[n, k, q]
        return jnp.concatenate([jnp.where(lo, v, zero), jnp.where(lo, zero, v)], axis=0)

    yb = [None] * 4
    for k in range(16):
        for q in range(4):
            v = dot_nt(r_ref[k, q], diag(0, k, q))
            if k:
                v = v - dot_nt(yb[q], diag(1, k, q))
            yb[q] = v.astype(BF)
            y_ref[k, q] = v
    zb = [None] * 4
    for k in reversed(range(16)):
        for q in range(4):
            v = y_ref[k, q]
            if k < 15:
                v = v - dot_nt(zb[q], diag(2, k, q))
            zb[q] = v.astype(BF)
            for d in range(4):
                w = k - 4 * d + 1
                if 0 <= w < 6:
                    z_ref[d, w, q] = zb[q]
    z_ref[0, 0] = jnp.zeros((4, 16, 128), BF)
    z_ref[3, 5] = jnp.zeros((4, 16, 128), BF)


def solve(r, f):
    return pl.pallas_call(
        s_kernel,
        out_shape=jax.ShapeDtypeStruct((4, 6, 4, 16, 128), BF),
        in_specs=[VM] * 2,
        out_specs=VM,
        scratch_shapes=[pltpu.VMEM((16, 4, 16, 128), F32)],
        compiler_params=pltpu.CompilerParams(vmem_limit_bytes=16 * 2**20),
        name="solve",
    )(r, f)


def inner_kernel(*refs, first):
    if first:
        own, kl, kh, b_ref, wbuf, xo, d2 = refs
    else:
        z, xg, b_ref, wbuf, xo, d2 = refs
    msk = inside()
    lo = lax.broadcasted_iota(jnp.int32, (16, 128), 1) < 64
    none = jnp.zeros((16, 128), BF)

    @pl.loop(0, 4)
    def _(i):
        for k in range(6):
            for jp in range(4):
                if not first:
                    v = xg[i, k, jp] + z[i, k, jp].astype(F32)
                elif k == 0:
                    v = jnp.where(msk[4], kl[i, jp], jnp.zeros((16, 128), F32))
                elif k == 5:
                    v = jnp.where(msk[5], kh[i, jp], jnp.zeros((16, 128), F32))
                else:
                    v = own[i, k - 1, jp]
                xo[i, k, jp] = v
                h = v.astype(BF)
                r = pltpu.roll(h, 64, 1)
                d2[1 + i, k, 1 + jp] = jnp.where(lo, h, r)
                d2[1 + i, k, 5 + jp] = jnp.where(lo, r, h)
            d2[1 + i, k, 0] = none
            d2[1 + i, k, 9] = none
        for k in range(1, 5):
            d2[0, k, 2 * i + 1] = none
            d2[0, k, 2 * i + 2] = none
            d2[5, k, 2 * i + 1] = none
            d2[5, k, 2 * i + 2] = none

    def gathered(i, k, j):
        return jnp.concatenate([
            jnp.where(lo, d2[i, k - 1, j], d2[i, k + 1, j]),
            jnp.where(lo, d2[i - 1, k, j], d2[i + 1, k, j]),
            jnp.where(lo, d2[i, k, j - 1], d2[i, k, j + 1]),
            d2[i, k, j]], axis=1)

    for i in range(4):
        for k in range(4):
            for jq in range(2):
                x = jnp.concatenate([gathered(i + 1, k + 1, 2 * jq + n + 4 * h + 1)
                                     for n in range(2) for h in range(2)], axis=0)
                w = jnp.concatenate([wbuf[f, 4 * i + k, 2 * jq:2 * jq + 2].reshape(256, 128)
                                     for f in range(4)], axis=1)
                o = dot_nt(x, w)
                for n in range(2):
                    jp = 2 * jq + n
                    cols = slice(128 * n, 128 * n + 128)
                    d = jnp.where(lo, o[32 * n:32 * n + 16, cols], o[32 * n + 16:32 * n + 32, cols])
                    xo[i, 6 + k, jp] = b_ref[i, k, jp] - d


def inner(state, b, w):
    first = len(state) == 3
    return pl.pallas_call(
        functools.partial(inner_kernel, first=first),
        out_shape=jax.ShapeDtypeStruct((4, 10, 4, 16, 128), F32),
        in_specs=[VM] * (len(state) + 2),
        out_specs=VM,
        scratch_shapes=[pltpu.VMEM((6, 6, 10, 16, 128), BF)],
        compiler_params=pltpu.CompilerParams(vmem_limit_bytes=24 * 2**20),
        cost_estimate=pl.CostEstimate(flops=2**27, bytes_accessed=2**24, transcendentals=0),
        name="inner",
    )(*state, b, w)


def outer_kernel(il, ih, jl, jh, part, w, out):
    msk = inside()
    lo = lax.broadcasted_iota(jnp.int32, (16, 128), 1) < 64
    none = jnp.zeros((16, 128), BF)

    def over_i(n, v, w):
        v = jnp.where(msk[n], v, none)
        r = pltpu.roll(v, 64, 1)
        if n == 0:
            x = jnp.concatenate([jnp.where(lo, v, none), jnp.where(lo, r, none)], axis=0)
        else:
            x = jnp.concatenate([jnp.where(lo, none, r), jnp.where(lo, none, v)], axis=0)
        o = dot_nt(x, w)
        return jnp.where(lo, o[:16], o[16:])

    def over_j(n, v, w):
        v = jnp.where(msk[2 + n], v, none)
        r = pltpu.roll(v, 64, 1)
        x = jnp.where(lo, r, none) if n == 0 else jnp.where(lo, none, r)
        o = dot_nt(x, w)
        return jnp.where(lo, o, 0.0) if n == 0 else jnp.where(lo, 0.0, o)

    for i in range(4):
        for k in range(4):
            for jp in range(4):
                v = part[i, 6 + k, jp]
                if i == 0:
                    v = v - over_i(0, il[k, jp], w[1, k, jp])
                if i == 3:
                    v = v - over_i(1, ih[k, jp], w[1, 12 + k, jp])
                if jp == 0:
                    v = v - over_j(0, jl[i, k], w[2, 4 * i + k, 0])
                if jp == 3:
                    v = v - over_j(1, jh[i, k], w[2, 4 * i + k, 3])
                out[i, k, jp] = v.astype(BF)


def outer(il, ih, jl, jh, part, w):
    return pl.pallas_call(
        outer_kernel,
        out_shape=jax.ShapeDtypeStruct((4, 4, 4, 16, 128), BF),
        in_specs=[VM] * 6,
        out_specs=VM,
        compiler_params=pltpu.CompilerParams(vmem_limit_bytes=24 * 2**20),
        name="outer",
    )(il, ih, jl, jh, part, w)


def inside():
    edges = []
    for axis in ("sx", "sy", "wn"):
        me = lax.axis_index(axis)
        edges += [me > 0, me < lax.axis_size(axis) - 1]
    return edges


def order_kernel(msc_hbm, x_hbm, own, ka, kb, ia, ib, ja, jb, msc, inv, x_ref, s_ref, sem):
    to_msc = pltpu.make_async_copy(msc_hbm, msc, sem.at[0])
    to_x = pltpu.make_async_copy(x_hbm, x_ref, sem.at[1])
    to_msc.start()
    to_x.start()
    lo = lax.broadcasted_iota(jnp.int32, (16, 128), 1) < 64
    to_msc.wait()
    slot = places(msc, inv)
    to_x.wait()
    spread(x_ref, s_ref)
    for i in range(4):
        for k in range(4):
            for jp in range(4):
                v = paired(s_ref, slot, i, k, jp, lo)
                h = v.astype(BF)
                own[i, k, jp] = v
                if k in (0, 3):
                    (ka if k == 0 else kb)[i, jp] = v
                if i in (0, 3):
                    (ia if i == 0 else ib)[k, jp] = h
                if jp in (0, 3):
                    (ja if jp == 0 else jb)[i, k] = h


def order(msc, x):
    wide = jax.ShapeDtypeStruct((4, 4, 16, 128), F32)
    side = jax.ShapeDtypeStruct((4, 4, 16, 128), BF)
    return pl.pallas_call(
        order_kernel,
        out_shape=(jax.ShapeDtypeStruct((4, 4, 4, 16, 128), F32), wide, wide) + (side,) * 4,
        in_specs=[HBM] * 2,
        out_specs=(VM,) * 7,
        scratch_shapes=[
            pltpu.SMEM((128,), jnp.int32),
            pltpu.SMEM((128,), jnp.int32),
            pltpu.VMEM((16, 64, 128), F32),
            pltpu.VMEM((16 * PITCH, 128), F32),
            pltpu.SemaphoreType.DMA((2,)),
        ],
        compiler_params=pltpu.CompilerParams(vmem_limit_bytes=8 * 2**20),
        name="order",
    )(*in_hbm(msc, x))


def sides_kernel(z, xg, ia, ib, ja, jb):
    for n in range(2):
        (ia, ib)[n][...] = (xg[3 * n, 1:5] + z[3 * n, 1:5].astype(F32)).astype(BF)
        (ja, jb)[n][...] = (xg[:, 1:5, 3 * n] + z[:, 1:5, 3 * n].astype(F32)).astype(BF)


def sides(z, xg):
    side = jax.ShapeDtypeStruct((4, 4, 16, 128), BF)
    return pl.pallas_call(
        sides_kernel,
        out_shape=(side,) * 4,
        in_specs=[VM, VM],
        out_specs=(VM,) * 4,
        compiler_params=pltpu.CompilerParams(vmem_limit_bytes=24 * 2**20),
        name="sides",
    )(z, xg)


def last_kernel(msc, row, z, xg, out, s_ref, inv):
    slot = places(msc, inv)
    for i in range(4):
        for k in range(4):
            for jp in range(4):
                v = xg[i, k + 1, jp] + z[i, k + 1, jp].astype(F32)
                s_ref[pl.ds(slot(i, k, jp), 16, stride=PITCH), :] = v
                s_ref[pl.ds(slot(i, k, jp + 4), 16, stride=PITCH), :] = v
    low = jnp.broadcast_to((row[...] & 4) == 0, (64, 128))
    for r in range(16):
        t = jnp.transpose(s_ref[pl.ds(r * PITCH, 128), :])
        out[r] = jnp.where(low, t[:64], t[64:])


def last(msc, row, z, xg):
    return pl.pallas_call(
        last_kernel,
        out_shape=jax.ShapeDtypeStruct((16, 64, 128), F32),
        in_specs=[pl.BlockSpec(memory_space=pltpu.SMEM)] + [VM] * 3,
        out_specs=VM,
        scratch_shapes=[pltpu.VMEM((16 * PITCH, 128), F32), pltpu.SMEM((128,), jnp.int32)],
        compiler_params=pltpu.CompilerParams(vmem_limit_bytes=8 * 2**20),
        name="last",
    )(msc, row, z, xg)


def shift(x, axis, d):
    n = lax.axis_size(axis)
    return lax.ppermute(x, axis, [(s, (s + d) % n) for s in range(n)])


def body(guess, forcing, msc, selfm, ifc, pm, gm, um):
    row = msc.reshape(1, 128)
    own, ka, kb, ia, ib, ja, jb = order(msc, guess)
    kl, kh = shift(kb, "wn", 1), shift(ka, "wn", -1)
    il, ih = shift(ib, "sx", 1), shift(ia, "sx", -1)
    jl, jh = shift(jb, "sy", 1), shift(ja, "sy", -1)
    b, w, f = prepare(msc, forcing, selfm, ifc, pm, gm, um)
    state = (own, kl, kh)
    for it in range(3):
        xg = inner(state, b, w)
        res = outer(il, ih, jl, jh, xg, w)
        lines = lax.all_to_all(res, "wn", 0, 0, tiled=True)
        z = solve(lines.reshape(16, 4, 16, 128), f)
        z = lax.all_to_all(z, "wn", 0, 0, tiled=True)
        if it < 2:
            ia, ib, ja, jb = sides(z, xg)
            il, ih = shift(ib, "sx", 1), shift(ia, "sx", -1)
            jl, jh = shift(jb, "sy", 1), shift(ja, "sy", -1)
            state = (z, xg)
    return last(msc, row, z, xg)


def solution(mesh):
    lastdim = P(None, None, ("sx", "sy", "wn"))
    return jax.shard_map(
        body,
        mesh=mesh,
        in_specs=(lastdim, lastdim, P(("sx", "sy", "wn")), lastdim,
                  P(None, None, None, ("sx", "sy", "wn")), lastdim, lastdim, lastdim),
        out_specs=lastdim,
        check_vma=False,
    )
```

```python
import functools

import jax
import jax.numpy as jnp
from jax import lax
from jax.experimental import pallas as pl
from jax.experimental.pallas import tpu as pltpu
from jax.sharding import PartitionSpec as P

BF = jnp.bfloat16
F32 = jnp.float32
VM = pl.BlockSpec(memory_space=pltpu.VMEM)
HBM = pl.BlockSpec(memory_space=pltpu.HBM)
NT = (((1,), (1,)), ((), ()))


def in_hbm(*arrays):
    return [pltpu.with_memory_space_constraint(a, pltpu.HBM) for a in arrays]


def dot_nt(a, b):
    return lax.dot_general(a, b, NT, preferred_element_type=F32)


PITCH = 129


def turn(buf, s_ref, a, b):
    @pl.loop(0, 64, unroll=64)
    def _(m):
        rows = jnp.concatenate([buf[a, m], buf[b, m]], axis=0)
        s_ref[pl.ds(m * PITCH, 128), :] = jnp.transpose(rows).astype(F32)


def picked(s_ref, s):
    return s_ref[pl.ds(s, 64, stride=PITCH), :].astype(BF)


def places(msc, inv):
    @pl.loop(0, 128, unroll=8)
    def _(s):
        inv[msc[s]] = s

    def slot(i, k, j):
        return inv[k * 32 + i * 8 + j]

    return slot


def spread(x_ref, s_ref):
    for r in range(16):
        x = x_ref[r]
        s_ref[pl.ds(r * PITCH, 128), :] = jnp.transpose(jnp.concatenate([x, x], axis=0))


def paired(s_ref, slot, i, k, jp, lo):
    return jnp.where(lo, s_ref[pl.ds(slot(i, k, jp), 16, stride=PITCH), :],
                     s_ref[pl.ds(slot(i, k, jp + 4), 16, stride=PITCH), :])


def prepare_kernel(msc_hbm, x_hbm, selfm, ifc, pm, gm, um, b_out, w_out, pg_out, u_out,
                   msc, inv, x_ref, buf, s_ref, sem):
    sources = [ifc.at[f] for f in range(6)] + [pm, gm, um, selfm]
    copies = [pltpu.make_async_copy(s, buf.at[n], sem.at[n]) for n, s in enumerate(sources)]
    to_msc = pltpu.make_async_copy(msc_hbm, msc, sem.at[10])
    to_x = pltpu.make_async_copy(x_hbm, x_ref, sem.at[11])
    for c in [to_msc, to_x] + copies:
        c.start()
    lo16 = lax.broadcasted_iota(jnp.int32, (16, 128), 1) < 64
    lo = lax.broadcasted_iota(jnp.int32, (64, 128), 1) < 64
    zero = jnp.zeros((64, 128), BF)
    to_msc.wait()
    slot = places(msc, inv)
    to_x.wait()
    spread(x_ref, s_ref)
    for i in range(4):
        for k in range(4):
            for jp in range(4):
                b_out[i, k, jp] = paired(s_ref, slot, i, k, jp, lo16)

    def put_element(t, s, v):
        c = msc[s]
        ik = (((c >> 3) & 3) << 2) | (c >> 5)
        half = pl.multiple_of(((c >> 2) & 1) << 6, 64)
        w_out[t, ik, c & 3, pl.ds(half, 64), :] = v

    for t in range(3):
        copies[2 * t].wait()
        copies[2 * t + 1].wait()
        turn(buf, s_ref, 2 * t, 2 * t + 1)

        @pl.loop(0, 128, unroll=32)
        def _(s):
            put_element(t, s, picked(s_ref, s))

    copies[6].wait()
    copies[7].wait()
    turn(buf, s_ref, 6, 7)

    @pl.loop(0, 16, unroll=4)
    def _(layer):
        for jp in range(4):
            v0 = picked(s_ref, layer * 8 + jp)
            pg_out[layer, jp, 0:64] = pltpu.roll(v0, 64, 1)
            pg_out[layer, jp, 64:128] = picked(s_ref, layer * 8 + jp + 4)

    copies[8].wait()
    copies[9].wait()
    turn(buf, s_ref, 8, 9)

    @pl.loop(0, 16, unroll=4)
    def _(layer):
        for jp in range(4):
            v0 = picked(s_ref, layer * 8 + jp)
            v1 = picked(s_ref, layer * 8 + jp + 4)
            u_out[layer, jp] = jnp.where(lo, v0, pltpu.roll(v1, 64, 1))
            put_element(3, layer * 8 + jp, jnp.where(lo, zero, v0))
            put_element(3, layer * 8 + jp + 4, jnp.where(lo, zero, v1))


def prepare(msc, x, selfm, ifc, pm, gm, um):
    return pl.pallas_call(
        prepare_kernel,
        out_shape=(jax.ShapeDtypeStruct((4, 4, 4, 16, 128), F32),
                   jax.ShapeDtypeStruct((4, 16, 4, 128, 128), BF),
                   jax.ShapeDtypeStruct((16, 4, 128, 128), BF),
                   jax.ShapeDtypeStruct((16, 4, 64, 128), BF)),
        in_specs=[HBM] * 7,
        out_specs=(VM,) * 4,
        scratch_shapes=[
            pltpu.SMEM((128,), jnp.int32),
            pltpu.SMEM((128,), jnp.int32),
            pltpu.VMEM((16, 64, 128), F32),
            pltpu.VMEM((10, 64, 64, 128), BF),
            pltpu.VMEM((64 * PITCH + 128, 128), F32),
            pltpu.SemaphoreType.DMA((12,)),
        ],
        compiler_params=pltpu.CompilerParams(vmem_limit_bytes=28 * 2**20),
        cost_estimate=pl.CostEstimate(flops=0, bytes_accessed=2**25, transcendentals=0),
        name="prepare",
    )(*in_hbm(msc, x, selfm, ifc, pm, gm, um))


def s_kernel(r_ref, pg_ref, u_ref, z_ref, y_ref):
    lo16 = lax.broadcasted_iota(jnp.int32, (16, 128), 1) < 64
    lo = lax.broadcasted_iota(jnp.int32, (64, 128), 1) < 64
    zero = jnp.zeros((64, 128), BF)
    minus = [jnp.zeros((16, 128), BF)] * 4
    for k in range(16):
        for q in range(4):
            r = pltpu.roll(r_ref[k, q], 64, 1)
            x = jnp.concatenate([jnp.where(lo16, minus[q], r), jnp.where(lo16, r, minus[q])], axis=0)
            o = dot_nt(x, pg_ref[k, q])
            v = jnp.where(lo16, o[:16], o[16:])
            minus[q] = (-v).astype(BF)
            y_ref[k, q] = v
    zb = [None] * 4
    for k in reversed(range(16)):
        for q in range(4):
            v = y_ref[k, q]
            if k < 15:
                u = u_ref[k, q]
                w = jnp.concatenate([jnp.where(lo, u, zero), jnp.where(lo, zero, u)], axis=0)
                v = v - dot_nt(zb[q], w)
            zb[q] = v.astype(BF)
            for d in range(4):
                w = k - 4 * d + 1
                if 0 <= w < 6:
                    z_ref[d, w, q] = zb[q]
    z_ref[0, 0] = jnp.zeros((4, 16, 128), BF)
    z_ref[3, 5] = jnp.zeros((4, 16, 128), BF)


def solve(r, pg, u):
    return pl.pallas_call(
        s_kernel,
        out_shape=jax.ShapeDtypeStruct((4, 6, 4, 16, 128), BF),
        in_specs=[VM] * 3,
        out_specs=VM,
        scratch_shapes=[pltpu.VMEM((16, 4, 16, 128), F32)],
        compiler_params=pltpu.CompilerParams(vmem_limit_bytes=16 * 2**20),
        name="solve",
    )(r, pg, u)


def inner_kernel(*refs, first):
    if first:
        own, kl, kh, b_ref, wbuf, xo, d2 = refs
    else:
        z, xg, b_ref, wbuf, xo, d2 = refs
    msk = inside()
    lo = lax.broadcasted_iota(jnp.int32, (16, 128), 1) < 64
    none = jnp.zeros((16, 128), BF)

    @pl.loop(0, 4)
    def _(i):
        for k in range(6):
            for jp in range(4):
                if not first:
                    v = xg[i, k, jp] + z[i, k, jp].astype(F32)
                elif k == 0:
                    v = jnp.where(msk[4], kl[i, jp], jnp.zeros((16, 128), F32))
                elif k == 5:
                    v = jnp.where(msk[5], kh[i, jp], jnp.zeros((16, 128), F32))
                else:
                    v = own[i, k - 1, jp]
                xo[i, k, jp] = v
                h = v.astype(BF)
                r = pltpu.roll(h, 64, 1)
                d2[1 + i, k, 1 + jp] = jnp.where(lo, h, r)
                d2[1 + i, k, 5 + jp] = jnp.where(lo, r, h)
            d2[1 + i, k, 0] = none
            d2[1 + i, k, 9] = none
        for k in range(1, 5):
            d2[0, k, 2 * i + 1] = none
            d2[0, k, 2 * i + 2] = none
            d2[5, k, 2 * i + 1] = none
            d2[5, k, 2 * i + 2] = none

    def gathered(i, k, j):
        return jnp.concatenate([
            jnp.where(lo, d2[i, k - 1, j], d2[i, k + 1, j]),
            jnp.where(lo, d2[i - 1, k, j], d2[i + 1, k, j]),
            jnp.where(lo, d2[i, k, j - 1], d2[i, k, j + 1]),
            d2[i, k, j]], axis=1)

    for i in range(4):
        for k in range(4):
            for jq in range(2):
                x = jnp.concatenate([gathered(i + 1, k + 1, 2 * jq + n + 4 * h + 1)
                                     for n in range(2) for h in range(2)], axis=0)
                w = jnp.concatenate([wbuf[f, 4 * i + k, 2 * jq:2 * jq + 2].reshape(256, 128)
                                     for f in range(4)], axis=1)
                o = dot_nt(x, w)
                for n in range(2):
                    jp = 2 * jq + n
                    cols = slice(128 * n, 128 * n + 128)
                    d = jnp.where(lo, o[32 * n:32 * n + 16, cols], o[32 * n + 16:32 * n + 32, cols])
                    xo[i, 6 + k, jp] = b_ref[i, k, jp] - d


def inner(state, b, w):
    first = len(state) == 3
    return pl.pallas_call(
        functools.partial(inner_kernel, first=first),
        out_shape=jax.ShapeDtypeStruct((4, 10, 4, 16, 128), F32),
        in_specs=[VM] * (len(state) + 2),
        out_specs=VM,
        scratch_shapes=[pltpu.VMEM((6, 6, 10, 16, 128), BF)],
        compiler_params=pltpu.CompilerParams(vmem_limit_bytes=24 * 2**20),
        cost_estimate=pl.CostEstimate(flops=2**27, bytes_accessed=2**24, transcendentals=0),
        name="inner",
    )(*state, b, w)


def outer_kernel(il, ih, jl, jh, part, w, out):
    msk = inside()
    lo = lax.broadcasted_iota(jnp.int32, (16, 128), 1) < 64
    none = jnp.zeros((16, 128), BF)

    def by_i(n, v):
        v = jnp.where(msk[n], v, none)
        r = pltpu.roll(v, 64, 1)
        if n == 0:
            return [jnp.where(lo, v, none), jnp.where(lo, r, none)]
        return [jnp.where(lo, none, r), jnp.where(lo, none, v)]

    def by_j(n, v):
        v = jnp.where(msk[2 + n], v, none)
        r = pltpu.roll(v, 64, 1)
        return jnp.where(lo, r, none) if n == 0 else jnp.where(lo, none, r)

    terms = {}
    for n, side in enumerate((il, ih)):
        for k in range(4):
            for jp in range(0, 4, 2):
                x = jnp.concatenate(by_i(n, side[k, jp]) + by_i(n, side[k, jp + 1]), axis=0)
                o = dot_nt(x, w[1, 12 * n + k, jp:jp + 2].reshape(256, 128))
                for t in range(2):
                    cols = slice(128 * t, 128 * t + 128)
                    d = jnp.where(lo, o[32 * t:32 * t + 16, cols], o[32 * t + 16:32 * t + 32, cols])
                    terms[3 * n, k, jp + t] = [d]
    for n, side in enumerate((jl, jh)):
        for i in range(4):
            for k in range(0, 4, 2):
                x = jnp.concatenate([by_j(n, side[i, k]), by_j(n, side[i, k + 1])], axis=0)
                o = dot_nt(x, jnp.concatenate([w[2, 4 * i + k, 3 * n], w[2, 4 * i + k + 1, 3 * n]], axis=0))
                for t in range(2):
                    d = o[16 * t:16 * t + 16, 128 * t:128 * t + 128]
                    d = jnp.where(lo, d, 0.0) if n == 0 else jnp.where(lo, 0.0, d)
                    terms.setdefault((i, k + t, 3 * n), []).append(d)
    for i in range(4):
        for k in range(4):
            for jp in range(4):
                v = part[i, 6 + k, jp]
                for d in terms.get((i, k, jp), []):
                    v = v - d
                out[i, k, jp] = v.astype(BF)


def outer(il, ih, jl, jh, part, w):
    return pl.pallas_call(
        outer_kernel,
        out_shape=jax.ShapeDtypeStruct((4, 4, 4, 16, 128), BF),
        in_specs=[VM] * 6,
        out_specs=VM,
        compiler_params=pltpu.CompilerParams(vmem_limit_bytes=24 * 2**20),
        name="outer",
    )(il, ih, jl, jh, part, w)


def inside():
    edges = []
    for axis in ("sx", "sy", "wn"):
        me = lax.axis_index(axis)
        edges += [me > 0, me < lax.axis_size(axis) - 1]
    return edges


def order_kernel(msc_hbm, x_hbm, own, ka, kb, ia, ib, ja, jb, msc, inv, x_ref, s_ref, sem):
    to_msc = pltpu.make_async_copy(msc_hbm, msc, sem.at[0])
    to_x = pltpu.make_async_copy(x_hbm, x_ref, sem.at[1])
    to_msc.start()
    to_x.start()
    lo = lax.broadcasted_iota(jnp.int32, (16, 128), 1) < 64
    to_msc.wait()
    slot = places(msc, inv)
    to_x.wait()
    spread(x_ref, s_ref)
    for i in range(4):
        for k in range(4):
            for jp in range(4):
                v = paired(s_ref, slot, i, k, jp, lo)
                h = v.astype(BF)
                own[i, k, jp] = v
                if k in (0, 3):
                    (ka if k == 0 else kb)[i, jp] = v
                if i in (0, 3):
                    (ia if i == 0 else ib)[k, jp] = h
                if jp in (0, 3):
                    (ja if jp == 0 else jb)[i, k] = h


def order(msc, x):
    wide = jax.ShapeDtypeStruct((4, 4, 16, 128), F32)
    side = jax.ShapeDtypeStruct((4, 4, 16, 128), BF)
    return pl.pallas_call(
        order_kernel,
        out_shape=(jax.ShapeDtypeStruct((4, 4, 4, 16, 128), F32), wide, wide) + (side,) * 4,
        in_specs=[HBM] * 2,
        out_specs=(VM,) * 7,
        scratch_shapes=[
            pltpu.SMEM((128,), jnp.int32),
            pltpu.SMEM((128,), jnp.int32),
            pltpu.VMEM((16, 64, 128), F32),
            pltpu.VMEM((16 * PITCH + 128, 128), F32),
            pltpu.SemaphoreType.DMA((2,)),
        ],
        compiler_params=pltpu.CompilerParams(vmem_limit_bytes=8 * 2**20),
        name="order",
    )(*in_hbm(msc, x))


def sides_kernel(z, xg, ia, ib, ja, jb):
    for n in range(2):
        (ia, ib)[n][...] = (xg[3 * n, 1:5] + z[3 * n, 1:5].astype(F32)).astype(BF)
        (ja, jb)[n][...] = (xg[:, 1:5, 3 * n] + z[:, 1:5, 3 * n].astype(F32)).astype(BF)


def sides(z, xg):
    side = jax.ShapeDtypeStruct((4, 4, 16, 128), BF)
    return pl.pallas_call(
        sides_kernel,
        out_shape=(side,) * 4,
        in_specs=[VM, VM],
        out_specs=(VM,) * 4,
        compiler_params=pltpu.CompilerParams(vmem_limit_bytes=24 * 2**20),
        name="sides",
    )(z, xg)


def last_kernel(msc, row, z, xg, out, s_ref, inv):
    slot = places(msc, inv)
    for i in range(4):
        for k in range(4):
            for jp in range(4):
                v = xg[i, k + 1, jp] + z[i, k + 1, jp].astype(F32)
                s_ref[pl.ds(slot(i, k, jp), 16, stride=PITCH), :] = v
                s_ref[pl.ds(slot(i, k, jp + 4), 16, stride=PITCH), :] = v
    low = jnp.broadcast_to((row[...] & 4) == 0, (64, 128))
    for r in range(16):
        t = jnp.transpose(s_ref[pl.ds(r * PITCH, 128), :])
        out[r] = jnp.where(low, t[:64], t[64:])


def last(msc, row, z, xg):
    return pl.pallas_call(
        last_kernel,
        out_shape=jax.ShapeDtypeStruct((16, 64, 128), F32),
        in_specs=[pl.BlockSpec(memory_space=pltpu.SMEM)] + [VM] * 3,
        out_specs=VM,
        scratch_shapes=[pltpu.VMEM((16 * PITCH + 128, 128), F32), pltpu.SMEM((128,), jnp.int32)],
        compiler_params=pltpu.CompilerParams(vmem_limit_bytes=8 * 2**20),
        name="last",
    )(msc, row, z, xg)


def shift(x, axis, d):
    n = lax.axis_size(axis)
    return lax.ppermute(x, axis, [(s, (s + d) % n) for s in range(n)])


def body(guess, forcing, msc, selfm, ifc, pm, gm, um):
    row = msc.reshape(1, 128)
    own, ka, kb, ia, ib, ja, jb = order(msc, guess)
    kl, kh = shift(kb, "wn", 1), shift(ka, "wn", -1)
    il, ih = shift(ib, "sx", 1), shift(ia, "sx", -1)
    jl, jh = shift(jb, "sy", 1), shift(ja, "sy", -1)
    b, w, pg, u = prepare(msc, forcing, selfm, ifc, pm, gm, um)
    state = (own, kl, kh)
    for it in range(3):
        xg = inner(state, b, w)
        res = outer(il, ih, jl, jh, xg, w)
        lines = lax.all_to_all(res, "wn", 0, 0, tiled=True)
        z = solve(lines.reshape(16, 4, 16, 128), pg, u)
        z = lax.all_to_all(z, "wn", 0, 0, tiled=True)
        if it < 2:
            ia, ib, ja, jb = sides(z, xg)
            il, ih = shift(ib, "sx", 1), shift(ia, "sx", -1)
            jl, jh = shift(jb, "sy", 1), shift(ja, "sy", -1)
            state = (z, xg)
    return last(msc, row, z, xg)


def solution(mesh):
    lastdim = P(None, None, ("sx", "sy", "wn"))
    return jax.shard_map(
        body,
        mesh=mesh,
        in_specs=(lastdim, lastdim, P(("sx", "sy", "wn")), lastdim,
                  P(None, None, None, ("sx", "sy", "wn")), lastdim, lastdim, lastdim),
        out_specs=lastdim,
        check_vma=False,
    )
```

```python
import functools

import jax
import jax.numpy as jnp
from jax import lax
from jax.experimental import pallas as pl
from jax.experimental.pallas import tpu as pltpu
from jax.sharding import PartitionSpec as P

BF = jnp.bfloat16
F32 = jnp.float32
VM = pl.BlockSpec(memory_space=pltpu.VMEM)
HBM = pl.BlockSpec(memory_space=pltpu.HBM)
NT = (((1,), (1,)), ((), ()))


def in_hbm(*arrays):
    return [pltpu.with_memory_space_constraint(a, pltpu.HBM) for a in arrays]


def dot_nt(a, b):
    return lax.dot_general(a, b, NT, preferred_element_type=F32)


PITCH = 129


def turn(buf, s_ref, a, b):
    @pl.loop(0, 64, unroll=64)
    def _(m):
        rows = jnp.concatenate([buf[a, m], buf[b, m]], axis=0)
        s_ref[pl.ds(m * PITCH, 128), :] = jnp.transpose(rows).astype(F32)


def picked(s_ref, s):
    return s_ref[pl.ds(s, 64, stride=PITCH), :].astype(BF)


def places(msc, inv):
    @pl.loop(0, 128, unroll=32)
    def _(s):
        inv[msc[s]] = s

    def slot(i, k, j):
        return inv[k * 32 + i * 8 + j]

    return slot


def spread(x_ref, s_ref):
    for r in range(16):
        x = x_ref[r]
        s_ref[pl.ds(r * PITCH, 128), :] = jnp.transpose(jnp.concatenate([x, x], axis=0))


def paired(s_ref, slot, i, k, jp, lo):
    return jnp.where(lo, s_ref[pl.ds(slot(i, k, jp), 16, stride=PITCH), :],
                     s_ref[pl.ds(slot(i, k, jp + 4), 16, stride=PITCH), :])


def prepare_kernel(msc_hbm, x_hbm, selfm, ifc, pm, gm, um, b_out, w_out, pg_out, u_out,
                   msc, inv, x_ref, buf, s_ref, sem):
    sources = [ifc.at[f] for f in range(6)] + [pm, gm, um, selfm]
    copies = [pltpu.make_async_copy(s, buf.at[n], sem.at[n]) for n, s in enumerate(sources)]
    to_msc = pltpu.make_async_copy(msc_hbm, msc, sem.at[10])
    to_x = pltpu.make_async_copy(x_hbm, x_ref, sem.at[11])
    for c in [to_msc, to_x] + copies:
        c.start()
    lo16 = lax.broadcasted_iota(jnp.int32, (16, 128), 1) < 64
    lo = lax.broadcasted_iota(jnp.int32, (64, 128), 1) < 64
    zero = jnp.zeros((64, 128), BF)
    to_msc.wait()
    slot = places(msc, inv)
    to_x.wait()
    spread(x_ref, s_ref)
    for i in range(4):
        for k in range(4):
            for jp in range(4):
                b_out[i, k, jp] = paired(s_ref, slot, i, k, jp, lo16)

    def put_element(t, s, v):
        c = msc[s]
        ik = (((c >> 3) & 3) << 2) | (c >> 5)
        half = pl.multiple_of(((c >> 2) & 1) << 6, 64)
        w_out[t, ik, c & 3, pl.ds(half, 64), :] = v

    for t in range(3):
        copies[2 * t].wait()
        copies[2 * t + 1].wait()
        turn(buf, s_ref, 2 * t, 2 * t + 1)

        @pl.loop(0, 128, unroll=64)
        def _(s):
            put_element(t, s, picked(s_ref, s))

    copies[6].wait()
    copies[7].wait()
    turn(buf, s_ref, 6, 7)

    @pl.loop(0, 16, unroll=8)
    def _(layer):
        for jp in range(4):
            v0 = picked(s_ref, layer * 8 + jp)
            pg_out[layer, jp, 0:64] = pltpu.roll(v0, 64, 1)
            pg_out[layer, jp, 64:128] = picked(s_ref, layer * 8 + jp + 4)

    copies[8].wait()
    copies[9].wait()
    turn(buf, s_ref, 8, 9)

    @pl.loop(0, 16, unroll=8)
    def _(layer):
        for jp in range(4):
            v0 = picked(s_ref, layer * 8 + jp)
            v1 = picked(s_ref, layer * 8 + jp + 4)
            u_out[layer, jp] = jnp.where(lo, v0, pltpu.roll(v1, 64, 1))
            put_element(3, layer * 8 + jp, jnp.where(lo, zero, v0))
            put_element(3, layer * 8 + jp + 4, jnp.where(lo, zero, v1))


def prepare(msc, x, selfm, ifc, pm, gm, um):
    return pl.pallas_call(
        prepare_kernel,
        out_shape=(jax.ShapeDtypeStruct((4, 4, 4, 16, 128), F32),
                   jax.ShapeDtypeStruct((4, 16, 4, 128, 128), BF),
                   jax.ShapeDtypeStruct((16, 4, 128, 128), BF),
                   jax.ShapeDtypeStruct((16, 4, 64, 128), BF)),
        in_specs=[HBM] * 7,
        out_specs=(VM,) * 4,
        scratch_shapes=[
            pltpu.SMEM((128,), jnp.int32),
            pltpu.SMEM((128,), jnp.int32),
            pltpu.VMEM((16, 64, 128), F32),
            pltpu.VMEM((10, 64, 64, 128), BF),
            pltpu.VMEM((64 * PITCH + 128, 128), F32),
            pltpu.SemaphoreType.DMA((12,)),
        ],
        compiler_params=pltpu.CompilerParams(vmem_limit_bytes=28 * 2**20),
        cost_estimate=pl.CostEstimate(flops=0, bytes_accessed=2**25, transcendentals=0),
        name="prepare",
    )(*in_hbm(msc, x, selfm, ifc, pm, gm, um))


def s_kernel(r_ref, pg_ref, u_ref, z_ref, y_ref):
    lo16 = lax.broadcasted_iota(jnp.int32, (16, 128), 1) < 64
    lo = lax.broadcasted_iota(jnp.int32, (64, 128), 1) < 64
    zero = jnp.zeros((64, 128), BF)
    minus = [jnp.zeros((16, 128), BF)] * 4
    for k in range(16):
        for q in range(4):
            r = pltpu.roll(r_ref[k, q], 64, 1)
            x = jnp.concatenate([jnp.where(lo16, minus[q], r), jnp.where(lo16, r, minus[q])], axis=0)
            o = dot_nt(x, pg_ref[k, q])
            v = jnp.where(lo16, o[:16], o[16:])
            minus[q] = (-v).astype(BF)
            y_ref[k, q] = v
    zb = [None] * 4
    for k in reversed(range(16)):
        for q in range(4):
            v = y_ref[k, q]
            if k < 15:
                u = u_ref[k, q]
                w = jnp.concatenate([jnp.where(lo, u, zero), jnp.where(lo, zero, u)], axis=0)
                v = v - dot_nt(zb[q], w)
            zb[q] = v.astype(BF)
            for d in range(4):
                w = k - 4 * d + 1
                if 0 <= w < 6:
                    z_ref[d, w, q] = zb[q]
    z_ref[0, 0] = jnp.zeros((4, 16, 128), BF)
    z_ref[3, 5] = jnp.zeros((4, 16, 128), BF)


def solve(r, pg, u):
    return pl.pallas_call(
        s_kernel,
        out_shape=jax.ShapeDtypeStruct((4, 6, 4, 16, 128), BF),
        in_specs=[VM] * 3,
        out_specs=VM,
        scratch_shapes=[pltpu.VMEM((16, 4, 16, 128), F32)],
        compiler_params=pltpu.CompilerParams(vmem_limit_bytes=16 * 2**20),
        name="solve",
    )(r, pg, u)


def inner_kernel(*refs, first):
    if first:
        own, kl, kh, b_ref, wbuf, xo, d2 = refs
    else:
        z, xg, b_ref, wbuf, xo, d2 = refs
    msk = inside()
    lo = lax.broadcasted_iota(jnp.int32, (16, 128), 1) < 64
    none = jnp.zeros((16, 128), BF)

    @pl.loop(0, 4)
    def _(i):
        for k in range(6):
            for jp in range(4):
                if not first:
                    v = xg[i, k, jp] + z[i, k, jp].astype(F32)
                elif k == 0:
                    v = jnp.where(msk[4], kl[i, jp], jnp.zeros((16, 128), F32))
                elif k == 5:
                    v = jnp.where(msk[5], kh[i, jp], jnp.zeros((16, 128), F32))
                else:
                    v = own[i, k - 1, jp]
                xo[i, k, jp] = v
                h = v.astype(BF)
                r = pltpu.roll(h, 64, 1)
                d2[1 + i, k, 1 + jp] = jnp.where(lo, h, r)
                d2[1 + i, k, 5 + jp] = jnp.where(lo, r, h)
            d2[1 + i, k, 0] = none
            d2[1 + i, k, 9] = none
        for k in range(1, 5):
            d2[0, k, 2 * i + 1] = none
            d2[0, k, 2 * i + 2] = none
            d2[5, k, 2 * i + 1] = none
            d2[5, k, 2 * i + 2] = none

    def gathered(i, k, j):
        return jnp.concatenate([
            jnp.where(lo, d2[i, k - 1, j], d2[i, k + 1, j]),
            jnp.where(lo, d2[i - 1, k, j], d2[i + 1, k, j]),
            jnp.where(lo, d2[i, k, j - 1], d2[i, k, j + 1]),
            d2[i, k, j]], axis=1)

    for i in range(4):
        for k in range(4):
            for jq in range(2):
                x = jnp.concatenate([gathered(i + 1, k + 1, 2 * jq + n + 4 * h + 1)
                                     for n in range(2) for h in range(2)], axis=0)
                w = jnp.concatenate([wbuf[f, 4 * i + k, 2 * jq:2 * jq + 2].reshape(256, 128)
                                     for f in range(4)], axis=1)
                o = dot_nt(x, w)
                for n in range(2):
                    jp = 2 * jq + n
                    cols = slice(128 * n, 128 * n + 128)
                    d = jnp.where(lo, o[32 * n:32 * n + 16, cols], o[32 * n + 16:32 * n + 32, cols])
                    xo[i, 6 + k, jp] = b_ref[i, k, jp] - d


def inner(state, b, w):
    first = len(state) == 3
    return pl.pallas_call(
        functools.partial(inner_kernel, first=first),
        out_shape=jax.ShapeDtypeStruct((4, 10, 4, 16, 128), F32),
        in_specs=[VM] * (len(state) + 2),
        out_specs=VM,
        scratch_shapes=[pltpu.VMEM((6, 6, 10, 16, 128), BF)],
        compiler_params=pltpu.CompilerParams(vmem_limit_bytes=24 * 2**20),
        cost_estimate=pl.CostEstimate(flops=2**27, bytes_accessed=2**24, transcendentals=0),
        name="inner",
    )(*state, b, w)


def outer_kernel(il, ih, jl, jh, part, w, out):
    msk = inside()
    lo = lax.broadcasted_iota(jnp.int32, (16, 128), 1) < 64
    none = jnp.zeros((16, 128), BF)

    def by_i(n, v):
        v = jnp.where(msk[n], v, none)
        r = pltpu.roll(v, 64, 1)
        if n == 0:
            return [jnp.where(lo, v, none), jnp.where(lo, r, none)]
        return [jnp.where(lo, none, r), jnp.where(lo, none, v)]

    def by_j(n, v):
        v = jnp.where(msk[2 + n], v, none)
        r = pltpu.roll(v, 64, 1)
        return jnp.where(lo, r, none) if n == 0 else jnp.where(lo, none, r)

    terms = {}
    for n, side in enumerate((il, ih)):
        for k in range(4):
            for jp in range(0, 4, 2):
                x = jnp.concatenate(by_i(n, side[k, jp]) + by_i(n, side[k, jp + 1]), axis=0)
                o = dot_nt(x, w[1, 12 * n + k, jp:jp + 2].reshape(256, 128))
                for t in range(2):
                    cols = slice(128 * t, 128 * t + 128)
                    d = jnp.where(lo, o[32 * t:32 * t + 16, cols], o[32 * t + 16:32 * t + 32, cols])
                    terms[3 * n, k, jp + t] = [d]
    for n, side in enumerate((jl, jh)):
        for i in range(4):
            for k in range(0, 4, 2):
                x = jnp.concatenate([by_j(n, side[i, k]), by_j(n, side[i, k + 1])], axis=0)
                o = dot_nt(x, jnp.concatenate([w[2, 4 * i + k, 3 * n], w[2, 4 * i + k + 1, 3 * n]], axis=0))
                for t in range(2):
                    d = o[16 * t:16 * t + 16, 128 * t:128 * t + 128]
                    d = jnp.where(lo, d, 0.0) if n == 0 else jnp.where(lo, 0.0, d)
                    terms.setdefault((i, k + t, 3 * n), []).append(d)
    for i in range(4):
        for k in range(4):
            for jp in range(4):
                v = part[i, 6 + k, jp]
                for d in terms.get((i, k, jp), []):
                    v = v - d
                out[i, k, jp] = v.astype(BF)


def outer(il, ih, jl, jh, part, w):
    return pl.pallas_call(
        outer_kernel,
        out_shape=jax.ShapeDtypeStruct((4, 4, 4, 16, 128), BF),
        in_specs=[VM] * 6,
        out_specs=VM,
        compiler_params=pltpu.CompilerParams(vmem_limit_bytes=24 * 2**20),
        name="outer",
    )(il, ih, jl, jh, part, w)


def inside():
    edges = []
    for axis in ("sx", "sy", "wn"):
        me = lax.axis_index(axis)
        edges += [me > 0, me < lax.axis_size(axis) - 1]
    return edges


def order_kernel(msc_hbm, x_hbm, own, ka, kb, ia, ib, ja, jb, msc, inv, x_ref, s_ref, sem):
    to_msc = pltpu.make_async_copy(msc_hbm, msc, sem.at[0])
    to_x = pltpu.make_async_copy(x_hbm, x_ref, sem.at[1])
    to_msc.start()
    to_x.start()
    lo = lax.broadcasted_iota(jnp.int32, (16, 128), 1) < 64
    to_msc.wait()
    slot = places(msc, inv)
    to_x.wait()
    spread(x_ref, s_ref)
    for i in range(4):
        for k in range(4):
            for jp in range(4):
                v = paired(s_ref, slot, i, k, jp, lo)
                h = v.astype(BF)
                own[i, k, jp] = v
                if k in (0, 3):
                    (ka if k == 0 else kb)[i, jp] = v
                if i in (0, 3):
                    (ia if i == 0 else ib)[k, jp] = h
                if jp in (0, 3):
                    (ja if jp == 0 else jb)[i, k] = h


def order(msc, x):
    wide = jax.ShapeDtypeStruct((4, 4, 16, 128), F32)
    side = jax.ShapeDtypeStruct((4, 4, 16, 128), BF)
    return pl.pallas_call(
        order_kernel,
        out_shape=(jax.ShapeDtypeStruct((4, 4, 4, 16, 128), F32), wide, wide) + (side,) * 4,
        in_specs=[HBM] * 2,
        out_specs=(VM,) * 7,
        scratch_shapes=[
            pltpu.SMEM((128,), jnp.int32),
            pltpu.SMEM((128,), jnp.int32),
            pltpu.VMEM((16, 64, 128), F32),
            pltpu.VMEM((16 * PITCH + 128, 128), F32),
            pltpu.SemaphoreType.DMA((2,)),
        ],
        compiler_params=pltpu.CompilerParams(vmem_limit_bytes=8 * 2**20),
        name="order",
    )(*in_hbm(msc, x))


def sides_kernel(z, xg, ia, ib, ja, jb):
    for n in range(2):
        (ia, ib)[n][...] = (xg[3 * n, 1:5] + z[3 * n, 1:5].astype(F32)).astype(BF)
        (ja, jb)[n][...] = (xg[:, 1:5, 3 * n] + z[:, 1:5, 3 * n].astype(F32)).astype(BF)


def sides(z, xg):
    side = jax.ShapeDtypeStruct((4, 4, 16, 128), BF)
    return pl.pallas_call(
        sides_kernel,
        out_shape=(side,) * 4,
        in_specs=[VM, VM],
        out_specs=(VM,) * 4,
        compiler_params=pltpu.CompilerParams(vmem_limit_bytes=24 * 2**20),
        name="sides",
    )(z, xg)


def last_kernel(msc, row, z, xg, out, s_ref, inv):
    slot = places(msc, inv)
    for i in range(4):
        for k in range(4):
            for jp in range(4):
                v = xg[i, k + 1, jp] + z[i, k + 1, jp].astype(F32)
                s_ref[pl.ds(slot(i, k, jp), 16, stride=PITCH), :] = v
                s_ref[pl.ds(slot(i, k, jp + 4), 16, stride=PITCH), :] = v
    low = jnp.broadcast_to((row[...] & 4) == 0, (64, 128))
    for r in range(16):
        t = jnp.transpose(s_ref[pl.ds(r * PITCH, 128), :])
        out[r] = jnp.where(low, t[:64], t[64:])


def last(msc, row, z, xg):
    return pl.pallas_call(
        last_kernel,
        out_shape=jax.ShapeDtypeStruct((16, 64, 128), F32),
        in_specs=[pl.BlockSpec(memory_space=pltpu.SMEM)] + [VM] * 3,
        out_specs=VM,
        scratch_shapes=[pltpu.VMEM((16 * PITCH + 128, 128), F32), pltpu.SMEM((128,), jnp.int32)],
        compiler_params=pltpu.CompilerParams(vmem_limit_bytes=8 * 2**20),
        name="last",
    )(msc, row, z, xg)


def shift(x, axis, d):
    n = lax.axis_size(axis)
    return lax.ppermute(x, axis, [(s, (s + d) % n) for s in range(n)])


def body(guess, forcing, msc, selfm, ifc, pm, gm, um):
    row = msc.reshape(1, 128)
    own, ka, kb, ia, ib, ja, jb = order(msc, guess)
    kl, kh = shift(kb, "wn", 1), shift(ka, "wn", -1)
    il, ih = shift(ib, "sx", 1), shift(ia, "sx", -1)
    jl, jh = shift(jb, "sy", 1), shift(ja, "sy", -1)
    b, w, pg, u = prepare(msc, forcing, selfm, ifc, pm, gm, um)
    state = (own, kl, kh)
    for it in range(3):
        xg = inner(state, b, w)
        res = outer(il, ih, jl, jh, xg, w)
        lines = lax.all_to_all(res, "wn", 0, 0, tiled=True)
        z = solve(lines.reshape(16, 4, 16, 128), pg, u)
        z = lax.all_to_all(z, "wn", 0, 0, tiled=True)
        if it < 2:
            ia, ib, ja, jb = sides(z, xg)
            il, ih = shift(ib, "sx", 1), shift(ia, "sx", -1)
            jl, jh = shift(jb, "sy", 1), shift(ja, "sy", -1)
            state = (z, xg)
    return last(msc, row, z, xg)


def solution(mesh):
    lastdim = P(None, None, ("sx", "sy", "wn"))
    return jax.shard_map(
        body,
        mesh=mesh,
        in_specs=(lastdim, lastdim, P(("sx", "sy", "wn")), lastdim,
                  P(None, None, None, ("sx", "sy", "wn")), lastdim, lastdim, lastdim),
        out_specs=lastdim,
        check_vma=False,
    )
```
